256 devices in a mesh: rank: 32 (over x, z), group: 8 (over y, core).
Axes of the slice: x: 4, y: 4, z: 8, core: 2. Of those that a mesh axis runs over, the one named last changes fastest.
Arguments:
- residual: bfloat16 [6144, 3584], P(('group', 'rank')), parts along dimension 0, may hold values from -6 to 6
- queries: bfloat16 [6144, 64, 576], P(('group', 'rank')), parts along dimension 0
- latent_cache: bfloat16 [6144, 128, 576], P(('group', 'rank')), parts along dimension 0
- lengths: int32 [6144], P(('group', 'rank')), parts along dimension 0, may hold values from 2 to 128, as said below
- counts: int32 [256], P('group'), parts along dimension 0, may hold values from 1 to 24, as said below
- value_up: bfloat16 [64, 512, 128], P('rank'), may hold values from -0.25 to 0.25
- out_proj: bfloat16 [8192, 3584], P('rank'), may hold values from -0.0625 to 0.0625
- norm_gain: bfloat16 [3584], replicated, may hold values from 0.5 to 1.5
- gate_up: bfloat16 [3584, 18432], P(None, 'rank'), may hold values from -0.09375 to 0.09375
- down_proj: bfloat16 [9216, 3584], P('rank'), may hold values from -0.0625 to 0.0625
Outputs:
- layer_out: bfloat16 [6144, 3584], P(('group', 'rank')), parts along dimension 0
The draws below stay inside these ranges and needn't reach their ends.
There are 8 independent parts, one for each index of `group`. The reference program is written for one: setup_inputs(seed, part) draws one part's arguments, and reference() takes and returns one part's arrays. A program takes and returns all parts, laid end to end along the dimension named above; an argument that names none is the same for every part. Nothing has to cross between parts.
Inputs may be any that keep to these rules, and one draw needn't show every extreme that they name: `counts`: some rank has all 24 slots live. `lengths`: some slot has the full 128 positions.
All inputs are finite; a program needn't handle non-finite values.
Results may differ from the reference program's by a relative error of at most 0.025.
Values may be sent and summed in bfloat16 or wider, within the bound.
No kernel may reach another device: no remote copies, remote signals or barrier semaphores. Data moves between devices by JAX's collectives and lax.ppermute only.
A program may use at most 128 MiB of HBM per device.

```python
import jax
import jax.numpy as jnp
from jax import lax

D = 3584
FF = 9216
HEADS = 64
LAT = 512
ROPE = 64
VDIM = 128
CAP = 24
LMAX = 128
ROWS = 768


def shared_cache(key):
    return jax.random.normal(key, (ROWS, LMAX, LAT + ROPE), jnp.float32)


def draw_latent_cache(key, part):
    base = shared_cache(key)
    return base.astype(jnp.bfloat16)


def draw_queries(key, part):
    key = jax.random.fold_in(key, 3)
    queries = jax.random.normal(key, (ROWS, HEADS, LAT + ROPE), jnp.float32)
    return queries.astype(jnp.bfloat16)


def draw_lengths(key, part):
    key = jax.random.fold_in(key, 5)
    first_key, second_key = jax.random.split(key)
    drawn = jax.random.randint(first_key, (ROWS,), 2, LMAX + 1, dtype=jnp.int32)
    chosen = jax.random.randint(second_key, (), 0, ROWS // CAP, dtype=jnp.int32) * CAP
    return drawn.at[chosen].set(LMAX)


def draw_counts(key, part):
    key = jax.random.fold_in(key, 9)
    first_key, second_key = jax.random.split(key)
    ranks = ROWS // CAP
    drawn = jax.random.randint(first_key, (ranks,), max(1, CAP // 4), CAP // 2 + 1, dtype=jnp.int32)
    chosen = jax.random.randint(second_key, (), 0, ranks, dtype=jnp.int32)
    return drawn.at[chosen].set(CAP)


def shard_levels(own_key, shape, pieces, smallest, top_value):
    gain = 1.0
    for dim, parts in pieces:
        heights = jax.random.uniform(jax.random.fold_in(jax.random.fold_in(own_key, 6), dim), (parts,), jnp.float32, smallest / len(pieces), top_value / len(pieces))
        gain = gain * jnp.repeat(jnp.exp(heights), shape[dim] // parts).reshape((-1,) + (1,) * (len(shape) - 1 - dim))
    return gain


def scatter_about(stream_key, extent, width, bound, shards=(), kind=jnp.bfloat16):
    factor_of = shard_levels(stream_key, extent, shards, -0.22, 0.18) if shards else 1.0
    entries = jax.random.normal(stream_key, extent, jnp.float32) * width * factor_of
    return jnp.minimum(jnp.maximum(entries, -bound), bound).astype(kind)


def setup_inputs(seed: int = 0, part: int = 0) -> dict:
    seeds = jax.random.split(jax.random.key(seed), 11)
    part_keys = jax.random.split(jax.random.fold_in(seeds[10], part), 11)
    return {
        "residual": scatter_about(part_keys[0], (ROWS, D), 1.0, 6.0, ((0, 32),)),
        "queries": draw_queries(jax.random.fold_in(jax.random.fold_in(seeds[10], part), 71), part),
        "latent_cache": draw_latent_cache(jax.random.fold_in(jax.random.fold_in(seeds[10], part), 71), part),
        "lengths": draw_lengths(jax.random.fold_in(jax.random.fold_in(seeds[10], part), 71), part),
        "counts": draw_counts(jax.random.fold_in(jax.random.fold_in(seeds[10], part), 71), part),
        "value_up": scatter_about(seeds[5], (HEADS, LAT, VDIM), LAT ** -0.5, 0.25, ((0, 32),)),
        "out_proj": scatter_about(seeds[6], (HEADS * VDIM, D), (HEADS * VDIM) ** -0.5, 0.0625, ((0, 32),)),
        "norm_gain": jnp.clip(1.0 + 0.1 * jax.random.normal(seeds[7], (D,), jnp.float32), 0.5, 1.5).astype(jnp.bfloat16),
        "gate_up": scatter_about(seeds[8], (D, 2 * FF), D ** -0.5, 0.09375, ((1, 32),)),
        "down_proj": scatter_about(seeds[9], (FF, D), FF ** -0.5, 0.0625, ((0, 32),)),
    }


def round_trip(values_in):
    return lax.optimization_barrier(values_in.astype(jnp.bfloat16)).astype(jnp.float32)

def normalize(stream, norm_gain):
    factor = lax.rsqrt(lax.optimization_barrier(jnp.mean(stream * stream, axis=-1, keepdims=True)) + 1e-06)
    return (stream * factor * norm_gain.astype(jnp.float32)).astype(jnp.bfloat16)

def block_sum(left_blocks, right_blocks, ranks, total_rows):

    def add_block(summed, index):
        term_rows = jnp.dot(left_blocks[:, index, :], right_blocks[index], preferred_element_type=jnp.float32)
        return (summed + round_trip(term_rows), None)
    start_sum = jnp.zeros((total_rows, right_blocks.shape[2]), jnp.float32)
    summed, _ = lax.scan(add_block, start_sum, jnp.arange(ranks, dtype=jnp.int32))
    return summed

def reference(residual, queries, latent_cache, lengths, counts, value_up, out_proj, norm_gain, gate_up, down_proj):
    total_rows = residual.shape[0]
    ranks = counts.shape[0]
    slots = total_rows // ranks
    row_ids = jnp.arange(total_rows, dtype=jnp.int32)
    alive_mask = row_ids % slots < counts[row_ids // slots]
    score_scale = (VDIM + ROPE) ** (-0.5)
    scores = jnp.einsum('shc,stc->sht', queries.astype(jnp.float32), latent_cache.astype(jnp.float32)) * score_scale
    in_range = jnp.arange(LMAX, dtype=jnp.int32)[None, None, :] < lengths[:, None, None]
    scores = jnp.where(in_range, scores, -1e+30)
    weights = jax.nn.softmax(scores, axis=-1).astype(jnp.bfloat16)
    latent = jnp.einsum('sht,stc->shc', weights.astype(jnp.float32), latent_cache[:, :, :LAT].astype(jnp.float32))
    latent = jnp.where(alive_mask[:, None, None], latent, 0.0).astype(jnp.bfloat16)
    values = jnp.einsum('shc,hcv->shv', latent.astype(jnp.float32), value_up.astype(jnp.float32)).astype(jnp.bfloat16)
    per_rank = HEADS // ranks
    value_blocks = values.reshape(total_rows, ranks, per_rank * VDIM)
    proj_blocks = out_proj.reshape(ranks, per_rank * VDIM, D)
    attention = block_sum(value_blocks, proj_blocks, ranks, total_rows)
    mixed = residual.astype(jnp.float32) + attention
    normed = normalize(mixed, norm_gain)
    hidden_width = FF // ranks
    split_weights = gate_up.reshape(D, ranks, 2, hidden_width)
    gate_part = jnp.dot(normed, split_weights[:, :, 0, :].reshape(D, FF), preferred_element_type=jnp.float32)
    up_part = jnp.dot(normed, split_weights[:, :, 1, :].reshape(D, FF), preferred_element_type=jnp.float32)
    hidden = (jax.nn.silu(gate_part) * up_part).astype(jnp.bfloat16)
    hidden_blocks = hidden.reshape(total_rows, ranks, hidden_width)
    down_blocks = down_proj.reshape(ranks, hidden_width, D)
    feed = block_sum(hidden_blocks, down_blocks, ranks, total_rows)
    return jnp.where(alive_mask[:, None], mixed + feed, 0.0).astype(jnp.bfloat16)
```

```python
import functools

import jax
import jax.numpy as jnp
from jax import lax
from jax.experimental import pallas as pl
from jax.experimental.pallas import tpu as pltpu
from jax.sharding import PartitionSpec as P

F32 = jnp.float32
BF16 = jnp.bfloat16
NX = 4
CAP = 384
CAP_Z = 64
EXTRA = 16
LANES = 128


def shift_x(ranks, k):
    nz = ranks // NX
    return [(x * nz + z, ((x + k) % NX) * nz + z) for x in range(NX) for z in range(nz)]


def shift_z(ranks, k):
    nz = ranks // NX
    return [(x * nz + z, x * nz + (z + k) % nz) for x in range(NX) for z in range(nz)]


def groups_x(ranks):
    nz = ranks // NX
    return [[x * nz + z for x in range(NX)] for z in range(nz)]


def groups_z(ranks):
    nz = ranks // NX
    return [[x * nz + z for z in range(nz)] for x in range(NX)]


def dot(a, b):
    return jnp.dot(a, b, preferred_element_type=F32)


def dot_nt(a, b):
    return lax.dot_general(a, b, (((1,), (1,)), ((), ())), preferred_element_type=F32)


def dot_tn(a, b):
    return lax.dot_general(a, b, (((0,), (0,)), ((), ())), preferred_element_type=F32)


def attend_kernel(scale, step_slots, lengths, queries, keys, out, *scratch):
    step = pl.program_id(0)
    slots, heads = out.shape[1], out.shape[0]
    latent_width = out.shape[2]
    positions = keys.shape[2]
    at = lax.broadcasted_iota(jnp.int32, (heads, positions), 1)
    for i in range(step_slots):
        slot = step * step_slots + i
        key = keys[i]
        scores = dot(queries[i], key) * scale
        scores = jnp.where(at < lengths[slot], scores, -1e30)
        weights = jnp.exp(scores - jnp.max(scores, axis=1, keepdims=True))
        weights = weights / jnp.sum(weights, axis=1, keepdims=True)
        latent = dot_nt(weights.astype(BF16), key[:latent_width])
        rows = pl.ds(pl.multiple_of(slot * heads, heads), heads)
        for lane, part in enumerate(scratch):
            part[rows, :] = latent[:, lane * LANES : (lane + 1) * LANES]

    @pl.when(step == pl.num_programs(0) - 1)
    def _():
        for head in range(heads):
            rows = [part[pl.ds(head, slots, stride=heads), :] for part in scratch]
            out[head] = jnp.concatenate(rows, axis=1).astype(BF16)


def attend(queries, latent_cache, lengths, latent_width, value_width):
    slots, heads, key_width = queries.shape
    positions = latent_cache.shape[1]
    rotary_width = key_width - latent_width
    scale = (value_width + rotary_width) ** (-0.5)
    step_slots = 4
    return pl.pallas_call(
        functools.partial(attend_kernel, scale, step_slots),
        out_shape=jax.ShapeDtypeStruct((heads, slots, latent_width), BF16),
        grid=(slots // step_slots,),
        in_specs=[
            pl.BlockSpec(memory_space=pltpu.SMEM),
            pl.BlockSpec((step_slots, heads, key_width), lambda i: (i, 0, 0)),
            pl.BlockSpec((step_slots, key_width, positions), lambda i: (i, 0, 0)),
        ],
        out_specs=pl.BlockSpec((heads, slots, latent_width), lambda i: (0, 0, 0)),
        scratch_shapes=[pltpu.VMEM((slots * heads, LANES), F32)] * (latent_width // LANES),
        compiler_params=pltpu.CompilerParams(vmem_limit_bytes=32 * 2**20),
        cost_estimate=pl.CostEstimate(
            flops=2 * slots * heads * positions * (key_width + latent_width),
            bytes_accessed=2 * slots * (heads + positions) * (key_width + latent_width),
            transcendentals=slots * heads * positions,
        ),
        name="attend",
    )(lengths, queries, latent_cache.transpose(0, 2, 1))


def down_kernel(terms, target, *refs):
    hiddens, downs, out = refs[:terms], refs[terms : 2 * terms], refs[2 * terms]
    total = dot_tn(hiddens[0][...], downs[0][...])
    for hidden, down in zip(hiddens[1:], downs[1:]):
        total = total + dot_tn(hidden[...], down[...])
    total = total.astype(BF16)
    nz, rows, _ = out.shape
    at = lax.broadcasted_iota(jnp.int32, (rows, total.shape[0]), 1)
    turn = lax.broadcasted_iota(jnp.int32, (rows, total.shape[0]), 0)
    for z in range(nz):
        pick = (at == turn + target[z]).astype(F32).astype(BF16)
        out[z] = dot(pick, total).astype(BF16)


def down_rows(hiddens, downs, first):
    nz = first.shape[0]
    cap = hiddens[0].shape[1]
    block = downs[0].shape[1]
    terms = len(hiddens)
    depth = sum(h.shape[0] for h in hiddens)
    return pl.pallas_call(
        functools.partial(down_kernel, terms),
        out_shape=jax.ShapeDtypeStruct((nz, CAP_Z, block), BF16),
        in_specs=[pl.BlockSpec(memory_space=pltpu.SMEM)]
        + [pl.BlockSpec(memory_space=pltpu.VMEM)] * (2 * terms),
        out_specs=pl.BlockSpec(memory_space=pltpu.VMEM),
        compiler_params=pltpu.CompilerParams(vmem_limit_bytes=32 * 2**20),
        cost_estimate=pl.CostEstimate(
            flops=2 * cap * block * (depth + nz * CAP_Z),
            bytes_accessed=2 * (depth * (cap + block) + nz * CAP_Z * block),
            transcendentals=0,
        ),
        name="down_rows",
    )(first, *hiddens, *downs)


def sends(ranks):
    return [shift_x(ranks, k) for k in range(1, NX)]


def take_cols(array, index, block):
    return lax.dynamic_slice_in_dim(array, index * block, block, 1)


def part_rows(height, members):
    rows = -(-height // (16 * members)) * 16
    while height % rows:
        rows += 16
    return rows


def exchange_weights(residual, out_proj, gate_up, down_proj, block):
    ranks = lax.axis_size("rank")
    members = lax.axis_size("group")
    member = lax.axis_index("group")
    my_x = lax.div(lax.axis_index("rank"), ranks // NX)
    matrices = [gate_up.T, down_proj, out_proj]
    parts = [part_rows(m.shape[0], members) for m in matrices]

    def cut(matrix, rows, x):
        piece = lax.dynamic_slice(matrix, (member * rows, x * block), (rows, block))
        return jnp.where(member * rows < matrix.shape[0], piece, jnp.zeros((), BF16))

    got = []
    for k in range(1, NX):
        x = lax.rem(my_x + k, NX)
        pieces = [cut(m, rows, x) for m, rows in zip(matrices, parts)]
        piece = jnp.concatenate(pieces + [take_cols(residual, x, block)], axis=0)
        got.append(lax.ppermute(piece, "rank", shift_x(ranks, k)))
    own = [take_cols(m, my_x, block) for m in matrices]
    res = [take_cols(residual, my_x, block)] + [g[sum(parts) :] for g in got]
    own[0] = jnp.pad(own[0], ((0, EXTRA), (0, 0)))
    return parts, got, own, jnp.concatenate(res, axis=0)


def gather_weights(parts, got, own):
    gathered, first = [], 0
    heights = [m.shape[0] for m in own]
    for height, rows in zip(heights, parts):
        piece = jnp.stack([g[first : first + rows] for g in got])
        gathered.append((height, piece))
        first += rows
    wholes = []
    for height, piece in gathered[::-1]:
        full = lax.all_gather(piece, "group", axis=1, tiled=True)
        full = jnp.pad(full, ((0, 0), (0, max(0, height - full.shape[1])), (0, 0)))
        wholes.append([full[k, :height] for k in range(NX - 1)])
    return [[m] + w for m, w in zip(own, wholes[::-1])]


def one_pass(index, values, res, joins, downs, outs, gain, place, base, width):
    ranks, slots = place.shape
    nz = ranks // NX
    block = gain.shape[0]
    rows_z = CAP // nz
    me = lax.axis_index("rank")
    my_x, my_z = lax.div(me, nz), lax.rem(me, nz)
    row = index * CAP + jnp.arange(CAP, dtype=jnp.int32)

    pick = (row[:, None] == place.reshape(-1)[None, :]).astype(BF16)
    packed = dot(pick, values).astype(BF16)
    heads = [packed] + [lax.ppermute(packed, "rank", perm) for perm in sends(ranks)]

    place_z = lax.dynamic_index_in_dim(place.reshape(NX, nz, slots), my_z, 1, False)
    order = lax.rem(my_x + NX - jnp.arange(NX, dtype=jnp.int32), NX)
    owners = place_z[order].reshape(-1)
    part = dot((row[:, None] == owners[None, :]).astype(BF16), res)
    for head, out in zip(heads, outs):
        part = part + dot(head, out)
    got = lax.all_to_all(
        part.astype(BF16).reshape(nz, rows_z, block),
        "rank",
        split_axis=0,
        concat_axis=0,
        tiled=True,
        axis_index_groups=groups_z(ranks),
    )
    mixed = jnp.sum(got.astype(F32), axis=0).astype(BF16)
    mixed = lax.all_to_all(
        jnp.broadcast_to(mixed[None], (nz, rows_z, block)),
        "rank",
        split_axis=0,
        concat_axis=0,
        tiled=True,
        axis_index_groups=groups_z(ranks),
    ).reshape(CAP, block)

    wide = mixed.astype(F32)
    square = jnp.sum(wide * wide, axis=1)
    high = lax.reduce_precision(square, 8, 7)
    both = joins[0].shape[0] - EXTRA
    line = jnp.arange(both + EXTRA, dtype=jnp.int32)[:, None]
    extra = jnp.where(line == both, high, jnp.where(line == both + 1, square - high, 0.0))
    scaled = (wide * gain[None, :]).astype(BF16)

    def share(join):
        return (dot_nt(join, scaled) + extra).astype(BF16)

    back = [shift_x(ranks, NX - k) for k in range(1, NX)]
    arrived = [lax.ppermute(share(join), "rank", perm) for join, perm in zip(joins[1:], back)]
    joined = share(joins[0]).astype(F32) + sum(a.astype(F32) for a in arrived)
    factor = lax.rsqrt((joined[both] + joined[both + 1]) / width + 1e-06)[None, :]
    gate, up = joined[: both // 2] * factor, joined[both // 2 : both] * factor
    hidden = (jax.nn.silu(gate) * up).astype(BF16)
    hiddens = [hidden] + [lax.ppermute(hidden, "rank", perm) for perm in sends(ranks)]

    sent = down_rows(hiddens, downs, base - index * CAP)
    got = lax.all_to_all(
        sent,
        "rank",
        split_axis=0,
        concat_axis=0,
        tiled=True,
        axis_index_groups=groups_z(ranks),
    )
    feed = jnp.sum(got.astype(F32), axis=0).astype(BF16)

    inside = (place_z >= index * CAP) & (place_z < (index + 1) * CAP)
    at = jnp.where(inside, place_z - base[my_z], -1).reshape(-1)
    take = (at[:, None] == jnp.arange(CAP_Z, dtype=jnp.int32)[None, :]).astype(BF16)
    keep = (place_z.reshape(-1)[:, None] == row[None, :]).astype(BF16)
    rows = (dot(take, feed) + dot(keep, mixed)).astype(BF16)
    rows = rows.reshape(NX, slots, block)
    pieces = [lax.dynamic_index_in_dim(rows, my_x, 0, False)] + [
        lax.ppermute(
            lax.dynamic_index_in_dim(rows, lax.rem(my_x + k, NX), 0, False),
            "rank",
            shift_x(ranks, k),
        )
        for k in range(1, NX)
    ]
    columns = []
    for x in range(NX):
        column = pieces[0]
        for k in range(1, NX):
            column = jnp.where(order[k] == x, pieces[k], column)
        columns.append(column)
    return jnp.concatenate(columns, axis=1), inside[my_x]


def packing(counts, slots):
    ranks = counts.shape[0]
    nz = ranks // NX
    grid = counts.reshape(NX, nz)
    before = jnp.cumsum(grid, axis=0) - grid
    total = jnp.sum(grid, axis=0)
    first = jnp.minimum(total, CAP_Z)
    rest = total - first
    passes = lax.div(jnp.sum(first) + CAP - 1, CAP)
    base_first = jnp.cumsum(first) - first
    base_rest = passes * CAP + jnp.cumsum(rest) - rest
    slot = jnp.arange(slots, dtype=jnp.int32)
    local = before[:, :, None] + slot
    place = jnp.where(
        local < CAP_Z, base_first[None, :, None] + local, base_rest[None, :, None] + local - CAP_Z
    )
    place = jnp.where(slot < grid[:, :, None], place, -1).reshape(ranks, slots)
    return place, base_first, base_rest, passes, passes + lax.div(jnp.sum(rest) + CAP - 1, CAP)


def per_device(
    residual,
    queries,
    latent_cache,
    lengths,
    counts,
    value_up,
    out_proj,
    norm_gain,
    gate_up,
    down_proj,
):
    slots = residual.shape[0]
    ranks = lax.axis_size("rank")
    latent_width, value_width = value_up.shape[1:]
    width = residual.shape[1]
    block = width // NX
    my_x = lax.div(lax.axis_index("rank"), ranks // NX)
    gain = lax.dynamic_slice_in_dim(norm_gain, my_x * block, block, 0).astype(F32)
    parts, got, own, res = exchange_weights(
        residual, out_proj, gate_up, down_proj, block
    )
    latent = attend(queries, latent_cache, lengths, latent_width, value_width)
    got = lax.optimization_barrier((got, latent))[0]
    joins, downs, outs = gather_weights(parts, got, own)
    arrived = lax.all_to_all(
        latent.reshape(ranks, -1, slots, latent_width), "rank", split_axis=0, concat_axis=0, tiled=True
    )
    arrived = arrived.transpose(0, 2, 1, 3).reshape(slots * ranks, -1, latent_width)
    values = jnp.einsum("shc,hcv->shv", arrived, value_up, preferred_element_type=F32)
    values = values.astype(BF16).reshape(slots * ranks, -1)
    place, base_first, base_rest, passes_first, passes = packing(counts, slots)

    def run(index):
        base = jnp.where(index < passes_first, base_first, base_rest)
        return one_pass(index, values, res, joins, downs, outs, gain, place, base, width)

    def more(state):
        index, out = state
        rows, inside = run(index)
        return index + 1, jnp.where(inside[:, None], rows, out)

    rows, inside = run(0)
    out = jnp.where(inside[:, None], rows, jnp.zeros((), BF16))
    return lax.while_loop(lambda state: state[0] < passes, more, (jnp.int32(1), out))[1]


def solution(mesh):
    placed = (
        P(("group", "rank"), None),
        P(("group", "rank"), None, None),
        P(("group", "rank"), None, None),
        P(("group", "rank")),
        P("group"),
        P("rank", None, None),
        P("rank", None),
        P(),
        P(None, "rank"),
        P("rank", None),
    )
    return jax.shard_map(
        per_device,
        mesh=mesh,
        in_specs=placed,
        out_specs=P(("group", "rank"), None),
        check_vma=False,
    )
```

```python
import functools

import jax
import jax.numpy as jnp
from jax import lax
from jax.experimental import pallas as pl
from jax.experimental.pallas import tpu as pltpu
from jax.sharding import PartitionSpec as P

F32 = jnp.float32
BF16 = jnp.bfloat16
NX = 4
CAP = 384
CAP_Z = 64
EXTRA = 16
LANES = 128


def shift_x(ranks, k):
    nz = ranks // NX
    return [(x * nz + z, ((x + k) % NX) * nz + z) for x in range(NX) for z in range(nz)]


def shift_z(ranks, k):
    nz = ranks // NX
    return [(x * nz + z, x * nz + (z + k) % nz) for x in range(NX) for z in range(nz)]


def groups_x(ranks):
    nz = ranks // NX
    return [[x * nz + z for x in range(NX)] for z in range(nz)]


def groups_z(ranks):
    nz = ranks // NX
    return [[x * nz + z for z in range(nz)] for x in range(NX)]


def dot(a, b):
    return jnp.dot(a, b, preferred_element_type=F32)


def dot_nt(a, b):
    return lax.dot_general(a, b, (((1,), (1,)), ((), ())), preferred_element_type=F32)


def dot_tn(a, b):
    return lax.dot_general(a, b, (((0,), (0,)), ((), ())), preferred_element_type=F32)


def attend_kernel(scale, step_slots, lengths, queries, keys, out, *scratch):
    step = pl.program_id(0)
    slots, heads = out.shape[1], out.shape[0]
    latent_width = out.shape[2]
    positions = keys.shape[2]
    at = lax.broadcasted_iota(jnp.int32, (heads, positions), 1)
    first = step * step_slots
    scores = [
        jnp.where(at < lengths[first + i], dot(queries[i], keys[i]) * scale, -1e30)
        for i in range(step_slots)
    ]
    scores = jnp.concatenate(scores, axis=0)
    weights = jnp.exp(scores - jnp.max(scores, axis=1, keepdims=True))
    weights = weights * (1.0 / jnp.sum(weights, axis=1, keepdims=True))
    weights = weights.astype(BF16)
    for i in range(step_slots):
        latent = dot_nt(weights[i * heads : (i + 1) * heads], keys[i, :latent_width])
        rows = pl.ds(pl.multiple_of((first + i) * heads, heads), heads)
        for lane, part in enumerate(scratch):
            part[rows, :] = latent[:, lane * LANES : (lane + 1) * LANES]

    @pl.when(step == pl.num_programs(0) - 1)
    def _():
        for head in range(heads):
            rows = [part[pl.ds(head, slots, stride=heads), :] for part in scratch]
            out[head] = jnp.concatenate(rows, axis=1).astype(BF16)


def attend(queries, latent_cache, lengths, latent_width, value_width):
    slots, heads, key_width = queries.shape
    positions = latent_cache.shape[1]
    rotary_width = key_width - latent_width
    scale = (value_width + rotary_width) ** (-0.5)
    step_slots = 8
    return pl.pallas_call(
        functools.partial(attend_kernel, scale, step_slots),
        out_shape=jax.ShapeDtypeStruct((heads, slots, latent_width), BF16),
        grid=(slots // step_slots,),
        in_specs=[
            pl.BlockSpec(memory_space=pltpu.SMEM),
            pl.BlockSpec((step_slots, heads, key_width), lambda i: (i, 0, 0)),
            pl.BlockSpec((step_slots, key_width, positions), lambda i: (i, 0, 0)),
        ],
        out_specs=pl.BlockSpec((heads, slots, latent_width), lambda i: (0, 0, 0)),
        scratch_shapes=[pltpu.VMEM((slots * heads, LANES), F32)] * (latent_width // LANES),
        compiler_params=pltpu.CompilerParams(vmem_limit_bytes=56 * 2**20),
        cost_estimate=pl.CostEstimate(
            flops=2 * slots * heads * positions * (key_width + latent_width),
            bytes_accessed=2 * slots * (heads + positions) * (key_width + latent_width),
            transcendentals=slots * heads * positions,
        ),
        name="attend",
    )(lengths, queries, latent_cache.transpose(0, 2, 1))


def down_kernel(terms, target, *refs):
    hiddens, downs, out = refs[:terms], refs[terms : 2 * terms], refs[2 * terms]
    total = dot_tn(hiddens[0][...], downs[0][...])
    for hidden, down in zip(hiddens[1:], downs[1:]):
        total = total + dot_tn(hidden[...], down[...])
    total = total.astype(BF16)
    nz, rows, _ = out.shape
    at = lax.broadcasted_iota(jnp.int32, (rows, total.shape[0]), 1)
    turn = lax.broadcasted_iota(jnp.int32, (rows, total.shape[0]), 0)
    for z in range(nz):
        pick = (at == turn + target[z]).astype(F32).astype(BF16)
        out[z] = dot(pick, total).astype(BF16)


def down_rows(hiddens, downs, first):
    nz = first.shape[0]
    cap = hiddens[0].shape[1]
    block = downs[0].shape[1]
    terms = len(hiddens)
    depth = sum(h.shape[0] for h in hiddens)
    return pl.pallas_call(
        functools.partial(down_kernel, terms),
        out_shape=jax.ShapeDtypeStruct((nz, CAP_Z, block), BF16),
        in_specs=[pl.BlockSpec(memory_space=pltpu.SMEM)]
        + [pl.BlockSpec(memory_space=pltpu.VMEM)] * (2 * terms),
        out_specs=pl.BlockSpec(memory_space=pltpu.VMEM),
        compiler_params=pltpu.CompilerParams(vmem_limit_bytes=32 * 2**20),
        cost_estimate=pl.CostEstimate(
            flops=2 * cap * block * (depth + nz * CAP_Z),
            bytes_accessed=2 * (depth * (cap + block) + nz * CAP_Z * block),
            transcendentals=0,
        ),
        name="down_rows",
    )(first, *hiddens, *downs)


def sends(ranks):
    return [shift_x(ranks, k) for k in range(1, NX)]


def take_cols(array, index, block):
    return lax.dynamic_slice_in_dim(array, index * block, block, 1)


def part_rows(height, members):
    rows = -(-height // (16 * members)) * 16
    while height % rows:
        rows += 16
    return rows


def exchange_weights(residual, out_proj, gate_up, down_proj, block):
    ranks = lax.axis_size("rank")
    members = lax.axis_size("group")
    member = lax.axis_index("group")
    my_x = lax.div(lax.axis_index("rank"), ranks // NX)
    matrices = [gate_up.T, down_proj, out_proj]
    parts = [part_rows(m.shape[0], members) for m in matrices]

    def cut(matrix, rows, x):
        piece = lax.dynamic_slice(matrix, (member * rows, x * block), (rows, block))
        return jnp.where(member * rows < matrix.shape[0], piece, jnp.zeros((), BF16))

    got = []
    for k in range(1, NX):
        x = lax.rem(my_x + k, NX)
        pieces = [cut(m, rows, x) for m, rows in zip(matrices, parts)]
        piece = jnp.concatenate(pieces + [take_cols(residual, x, block)], axis=0)
        got.append(lax.ppermute(piece, "rank", shift_x(ranks, k)))
    res = [take_cols(residual, my_x, block)] + [g[sum(parts) :] for g in got]
    return parts, got, matrices, jnp.concatenate(res, axis=0)


def gather_weights(parts, got):
    gathered, first = [], 0
    for rows in parts:
        gathered.append(jnp.stack([g[first : first + rows] for g in got]))
        first += rows
    return [lax.all_gather(g, "group", axis=1, tiled=True) for g in gathered[::-1]][::-1]


def own_blocks(matrices, my_x, block):
    blocks = [take_cols(m, my_x, block) for m in matrices]
    return [jnp.pad(blocks[0], ((0, EXTRA), (0, 0)))] + blocks[1:]


def weight_blocks(own, gathered):
    blocks = []
    for mine, full in zip(own, gathered):
        height = mine.shape[0]
        full = jnp.pad(full, ((0, 0), (0, max(0, height - full.shape[1])), (0, 0)))
        blocks.append([mine] + [full[k, :height] for k in range(NX - 1)])
    return blocks


def one_pass(index, values, res, own, gathered, gain, place, base, width):
    ranks, slots = place.shape
    nz = ranks // NX
    block = gain.shape[0]
    rows_z = CAP // nz
    me = lax.axis_index("rank")
    my_x, my_z = lax.div(me, nz), lax.rem(me, nz)
    joins, downs, outs = weight_blocks(own, gathered)
    row = index * CAP + jnp.arange(CAP, dtype=jnp.int32)

    pick = (row[:, None] == place.reshape(-1)[None, :]).astype(BF16)
    packed = dot(pick, values).astype(BF16)
    heads = [packed] + [lax.ppermute(packed, "rank", perm) for perm in sends(ranks)]

    place_z = lax.dynamic_index_in_dim(place.reshape(NX, nz, slots), my_z, 1, False)
    order = lax.rem(my_x + NX - jnp.arange(NX, dtype=jnp.int32), NX)
    owners = place_z[order].reshape(-1)
    part = dot((row[:, None] == owners[None, :]).astype(BF16), res)
    for head, out in zip(heads, outs):
        part = part + dot(head, out)
    got = lax.all_to_all(
        part.astype(BF16).reshape(nz, rows_z, block),
        "rank",
        split_axis=0,
        concat_axis=0,
        tiled=True,
        axis_index_groups=groups_z(ranks),
    )
    mixed = jnp.sum(got.astype(F32), axis=0).astype(BF16)
    mixed = lax.all_to_all(
        jnp.broadcast_to(mixed[None], (nz, rows_z, block)),
        "rank",
        split_axis=0,
        concat_axis=0,
        tiled=True,
        axis_index_groups=groups_z(ranks),
    ).reshape(CAP, block)

    wide = mixed.astype(F32)
    square = jnp.sum(wide * wide, axis=1)
    high = lax.reduce_precision(square, 8, 7)
    both = joins[0].shape[0] - EXTRA
    line = jnp.arange(both + EXTRA, dtype=jnp.int32)[:, None]
    extra = jnp.where(line == both, high, jnp.where(line == both + 1, square - high, 0.0))
    scaled = (wide * gain[None, :]).astype(BF16)

    def share(join):
        return (dot_nt(join, scaled) + extra).astype(BF16)

    back = [shift_x(ranks, NX - k) for k in range(1, NX)]
    arrived = [lax.ppermute(share(join), "rank", perm) for join, perm in zip(joins[1:], back)]
    joined = share(joins[0]).astype(F32) + sum(a.astype(F32) for a in arrived)
    factor = lax.rsqrt((joined[both] + joined[both + 1]) / width + 1e-06)[None, :]
    gate, up = joined[: both // 2] * factor, joined[both // 2 : both] * factor
    hidden = (jax.nn.silu(gate) * up).astype(BF16)
    hiddens = [hidden] + [lax.ppermute(hidden, "rank", perm) for perm in sends(ranks)]

    sent = down_rows(hiddens, downs, base - index * CAP)
    got = lax.all_to_all(
        sent,
        "rank",
        split_axis=0,
        concat_axis=0,
        tiled=True,
        axis_index_groups=groups_z(ranks),
    )
    feed = jnp.sum(got.astype(F32), axis=0).astype(BF16)

    inside = (place_z >= index * CAP) & (place_z < (index + 1) * CAP)
    at = jnp.where(inside, place_z - base[my_z], -1).reshape(-1)
    take = (at[:, None] == jnp.arange(CAP_Z, dtype=jnp.int32)[None, :]).astype(BF16)
    keep = (place_z.reshape(-1)[:, None] == row[None, :]).astype(BF16)
    rows = (dot(take, feed) + dot(keep, mixed)).astype(BF16)
    rows = rows.reshape(NX, slots, block)
    pieces = [lax.dynamic_index_in_dim(rows, my_x, 0, False)] + [
        lax.ppermute(
            lax.dynamic_index_in_dim(rows, lax.rem(my_x + k, NX), 0, False),
            "rank",
            shift_x(ranks, k),
        )
        for k in range(1, NX)
    ]
    columns = []
    for x in range(NX):
        column = pieces[0]
        for k in range(1, NX):
            column = jnp.where(order[k] == x, pieces[k], column)
        columns.append(column)
    return jnp.concatenate(columns, axis=1), inside[my_x]


def packing(counts, slots):
    ranks = counts.shape[0]
    nz = ranks // NX
    grid = counts.reshape(NX, nz)
    before = jnp.cumsum(grid, axis=0) - grid
    total = jnp.sum(grid, axis=0)
    first = jnp.minimum(total, CAP_Z)
    rest = total - first
    passes = lax.div(jnp.sum(first) + CAP - 1, CAP)
    base_first = jnp.cumsum(first) - first
    base_rest = passes * CAP + jnp.cumsum(rest) - rest
    slot = jnp.arange(slots, dtype=jnp.int32)
    local = before[:, :, None] + slot
    place = jnp.where(
        local < CAP_Z, base_first[None, :, None] + local, base_rest[None, :, None] + local - CAP_Z
    )
    place = jnp.where(slot < grid[:, :, None], place, -1).reshape(ranks, slots)
    return place, base_first, base_rest, passes, passes + lax.div(jnp.sum(rest) + CAP - 1, CAP)


def per_device(
    residual,
    queries,
    latent_cache,
    lengths,
    counts,
    value_up,
    out_proj,
    norm_gain,
    gate_up,
    down_proj,
):
    slots = residual.shape[0]
    ranks = lax.axis_size("rank")
    latent_width, value_width = value_up.shape[1:]
    width = residual.shape[1]
    block = width // NX
    my_x = lax.div(lax.axis_index("rank"), ranks // NX)
    gain = lax.dynamic_slice_in_dim(norm_gain, my_x * block, block, 0).astype(F32)
    parts, got, own, res = exchange_weights(residual, out_proj, gate_up, down_proj, block)
    latent = attend(queries, latent_cache, lengths, latent_width, value_width)
    got = lax.optimization_barrier((got, latent))[0]
    gathered = gather_weights(parts, got)
    own = own_blocks(own, my_x, block)
    arrived = lax.all_to_all(
        latent.reshape(ranks, -1, slots, latent_width), "rank", split_axis=0, concat_axis=0, tiled=True
    )
    arrived = arrived.transpose(0, 2, 1, 3).reshape(slots * ranks, -1, latent_width)
    values = jnp.einsum("shc,hcv->shv", arrived, value_up, preferred_element_type=F32)
    values = values.astype(BF16).reshape(slots * ranks, -1)
    place, base_first, base_rest, passes_first, passes = packing(counts, slots)

    def run(index):
        base = jnp.where(index < passes_first, base_first, base_rest)
        return one_pass(index, values, res, own, gathered, gain, place, base, width)

    def more(state):
        index, out = state
        rows, inside = run(index)
        return index + 1, jnp.where(inside[:, None], rows, out)

    rows, inside = run(0)
    out = jnp.where(inside[:, None], rows, jnp.zeros((), BF16))
    return lax.while_loop(lambda state: state[0] < passes, more, (jnp.int32(1), out))[1]


def solution(mesh):
    placed = (
        P(("group", "rank"), None),
        P(("group", "rank"), None, None),
        P(("group", "rank"), None, None),
        P(("group", "rank")),
        P("group"),
        P("rank", None, None),
        P("rank", None),
        P(),
        P(None, "rank"),
        P("rank", None),
    )
    return jax.shard_map(
        per_device,
        mesh=mesh,
        in_specs=placed,
        out_specs=P(("group", "rank"), None),
        check_vma=False,
    )
```

```python
import functools

import jax
import jax.numpy as jnp
from jax import lax
from jax.experimental import pallas as pl
from jax.experimental.pallas import tpu as pltpu
from jax.sharding import PartitionSpec as P

F32 = jnp.float32
BF16 = jnp.bfloat16
NX = 4
CAP = 384
CAP_Z = 64
EXTRA = 16
LANES = 128


def shift_x(ranks, k):
    nz = ranks // NX
    return [(x * nz + z, ((x + k) % NX) * nz + z) for x in range(NX) for z in range(nz)]


def shift_z(ranks, k):
    nz = ranks // NX
    return [(x * nz + z, x * nz + (z + k) % nz) for x in range(NX) for z in range(nz)]


def groups_x(ranks):
    nz = ranks // NX
    return [[x * nz + z for x in range(NX)] for z in range(nz)]


def groups_z(ranks):
    nz = ranks // NX
    return [[x * nz + z for z in range(nz)] for x in range(NX)]


def dot(a, b):
    return jnp.dot(a, b, preferred_element_type=F32)


def dot_nt(a, b):
    return lax.dot_general(a, b, (((1,), (1,)), ((), ())), preferred_element_type=F32)


def dot_tn(a, b):
    return lax.dot_general(a, b, (((0,), (0,)), ((), ())), preferred_element_type=F32)


def attend_kernel(scale, step_slots, lengths, queries, keys, out, *scratch):
    step = pl.program_id(0)
    slots, heads = out.shape[1], out.shape[0]
    latent_width = out.shape[2]
    positions = keys.shape[2]
    at = lax.broadcasted_iota(jnp.int32, (heads, positions), 1)
    first = step * step_slots
    scores = [
        jnp.where(at < lengths[first + i], dot(queries[i], keys[i]) * scale, -1e30)
        for i in range(step_slots)
    ]
    scores = jnp.concatenate(scores, axis=0)
    weights = jnp.exp(scores - jnp.max(scores, axis=1, keepdims=True))
    weights = weights * (1.0 / jnp.sum(weights, axis=1, keepdims=True))
    weights = weights.astype(BF16)
    for i in range(step_slots):
        latent = dot_nt(weights[i * heads : (i + 1) * heads], keys[i, :latent_width])
        rows = pl.ds(pl.multiple_of((first + i) * heads, heads), heads)
        for lane, part in enumerate(scratch):
            part[rows, :] = latent[:, lane * LANES : (lane + 1) * LANES]

    @pl.when(step == pl.num_programs(0) - 1)
    def _():
        for head in range(heads):
            rows = [part[pl.ds(head, slots, stride=heads), :] for part in scratch]
            out[head] = jnp.concatenate(rows, axis=1).astype(BF16)


def attend(queries, latent_cache, lengths, latent_width, value_width):
    slots, heads, key_width = queries.shape
    positions = latent_cache.shape[1]
    rotary_width = key_width - latent_width
    scale = (value_width + rotary_width) ** (-0.5)
    step_slots = 8
    return pl.pallas_call(
        functools.partial(attend_kernel, scale, step_slots),
        out_shape=jax.ShapeDtypeStruct((heads, slots, latent_width), BF16),
        grid=(slots // step_slots,),
        in_specs=[
            pl.BlockSpec(memory_space=pltpu.SMEM),
            pl.BlockSpec((step_slots, heads, key_width), lambda i: (i, 0, 0)),
            pl.BlockSpec((step_slots, key_width, positions), lambda i: (i, 0, 0)),
        ],
        out_specs=pl.BlockSpec((heads, slots, latent_width), lambda i: (0, 0, 0)),
        scratch_shapes=[pltpu.VMEM((slots * heads, LANES), F32)] * (latent_width // LANES),
        compiler_params=pltpu.CompilerParams(vmem_limit_bytes=56 * 2**20),
        cost_estimate=pl.CostEstimate(
            flops=2 * slots * heads * positions * (key_width + latent_width),
            bytes_accessed=2 * slots * (heads + positions) * (key_width + latent_width),
            transcendentals=slots * heads * positions,
        ),
        name="attend",
    )(lengths, queries, latent_cache.transpose(0, 2, 1))


def values_kernel(terms, local, *refs):
    latents, value_up, out = refs[:terms], refs[terms], refs[terms + 1]
    heads = value_up.shape[0]
    value_width = value_up.shape[2]
    blocks, rows, _ = out.shape
    slots = local.shape[1]
    turn = lax.broadcasted_iota(jnp.int32, (rows, slots), 0)
    pick = (turn == local[...]).astype(F32).astype(BF16)
    for head in range(heads):
        latent = jnp.concatenate([ref[head].astype(F32) for ref in latents], axis=0)
        values = dot(latent.astype(BF16), value_up[head]).astype(BF16)
        each = heads // blocks
        columns = slice(head % each * value_width, (head % each + 1) * value_width)
        out[head // each, :, columns] = dot(pick, values).astype(BF16)


def packed_values(latents, value_up, local, blocks):
    heads, slots, latent_width = latents[0].shape
    value_width = value_up.shape[2]
    terms = len(latents)
    macs = terms * slots * heads * (latent_width + CAP_Z) * value_width
    return pl.pallas_call(
        functools.partial(values_kernel, terms),
        out_shape=jax.ShapeDtypeStruct((blocks, CAP_Z, heads // blocks * value_width), BF16),
        in_specs=[pl.BlockSpec(memory_space=pltpu.VMEM)] * (terms + 2),
        out_specs=pl.BlockSpec(memory_space=pltpu.VMEM),
        compiler_params=pltpu.CompilerParams(vmem_limit_bytes=32 * 2**20),
        cost_estimate=pl.CostEstimate(
            flops=2 * macs,
            bytes_accessed=2 * heads * (terms * slots + value_width) * latent_width,
            transcendentals=0,
        ),
        name="packed_values",
    )(local[None], *latents, value_up)


def down_kernel(terms, target, *refs):
    hiddens, downs, out = refs[:terms], refs[terms : 2 * terms], refs[2 * terms]
    total = dot_tn(hiddens[0][...], downs[0][...])
    for hidden, down in zip(hiddens[1:], downs[1:]):
        total = total + dot_tn(hidden[...], down[...])
    total = total.astype(BF16)
    nz, rows, _ = out.shape
    at = lax.broadcasted_iota(jnp.int32, (rows, total.shape[0]), 1)
    turn = lax.broadcasted_iota(jnp.int32, (rows, total.shape[0]), 0)
    for z in range(nz):
        pick = (at == turn + target[z]).astype(F32).astype(BF16)
        out[z] = dot(pick, total).astype(BF16)


def down_rows(hiddens, downs, first):
    nz = first.shape[0]
    cap = hiddens[0].shape[1]
    block = downs[0].shape[1]
    terms = len(hiddens)
    depth = sum(h.shape[0] for h in hiddens)
    return pl.pallas_call(
        functools.partial(down_kernel, terms),
        out_shape=jax.ShapeDtypeStruct((nz, CAP_Z, block), BF16),
        in_specs=[pl.BlockSpec(memory_space=pltpu.SMEM)]
        + [pl.BlockSpec(memory_space=pltpu.VMEM)] * (2 * terms),
        out_specs=pl.BlockSpec(memory_space=pltpu.VMEM),
        compiler_params=pltpu.CompilerParams(vmem_limit_bytes=32 * 2**20),
        cost_estimate=pl.CostEstimate(
            flops=2 * cap * block * (depth + nz * CAP_Z),
            bytes_accessed=2 * (depth * (cap + block) + nz * CAP_Z * block),
            transcendentals=0,
        ),
        name="down_rows",
    )(first, *hiddens, *downs)


def sends(ranks):
    return [shift_x(ranks, k) for k in range(1, NX)]


def take_cols(array, index, block):
    return lax.dynamic_slice_in_dim(array, index * block, block, 1)


def part_rows(height, members):
    rows = -(-height // (16 * members)) * 16
    while height % rows:
        rows += 16
    return rows


def exchange_parts(matrices, wholes, member, block):
    ranks = lax.axis_size("rank")
    members = lax.axis_size("group")
    my_x = lax.div(lax.axis_index("rank"), ranks // NX)
    parts = [part_rows(m.shape[0], members) for m in matrices]

    def cut(matrix, rows, x):
        piece = lax.dynamic_slice(matrix, (member * rows, x * block), (rows, block))
        return jnp.where(member * rows < matrix.shape[0], piece, jnp.zeros((), BF16))

    got = []
    for k in range(1, NX):
        x = lax.rem(my_x + k, NX)
        pieces = [cut(m, rows, x) for m, rows in zip(matrices, parts)]
        pieces += [take_cols(m, x, block) for m in wholes]
        got.append(lax.ppermute(jnp.concatenate(pieces, axis=0), "rank", shift_x(ranks, k)))
    return parts, got


def gather_parts(parts, got):
    gathered, first = [], 0
    for rows in parts:
        gathered.append(jnp.stack([g[first : first + rows] for g in got]))
        first += rows
    return [lax.all_gather(g, "group", axis=1, tiled=True) for g in gathered]


def weight_blocks(mine, full):
    height = mine.shape[0]
    full = jnp.pad(full, ((0, 0), (0, max(0, height - full.shape[1])), (0, 0)))
    return [mine] + [full[k, :height] for k in range(NX - 1)]


def x_order(my_x):
    return lax.rem(my_x + NX - jnp.arange(NX, dtype=jnp.int32), NX)


def at_z(array, my_z):
    return lax.dynamic_index_in_dim(array, my_z, 1, False)


def local_values(index, latents, value_up, pack):
    local, _, _, passes_first = pack[1:5]
    ranks = lax.axis_size("rank")
    nz = ranks // NX
    me = lax.axis_index("rank")
    my_x, my_z = lax.div(me, nz), lax.rem(me, nz)
    mine = at_z(local, my_z)[x_order(my_x)].reshape(-1)
    mine = mine - jnp.where(index < passes_first, 0, CAP_Z)
    return packed_values(latents, value_up, mine, nz)


def project(index, sent, res, outs, pack):
    place, _, counted, bases, passes_first = pack
    ranks, slots = place.shape
    nz = ranks // NX
    me = lax.axis_index("rank")
    my_x, my_z = lax.div(me, nz), lax.rem(me, nz)
    row = index * CAP + jnp.arange(CAP, dtype=jnp.int32)
    got = lax.all_to_all(
        sent, "rank", split_axis=0, concat_axis=0, tiled=True, axis_index_groups=groups_z(ranks)
    )

    turn = jnp.arange(CAP_Z, dtype=jnp.int32)
    which = jnp.where(index < passes_first, 0, 1)
    target = jnp.where(turn < counted[which][:, None], bases[which][:, None] + turn, -1)
    pick = (row[:, None] == target.reshape(-1)[None, :]).astype(BF16)
    packed = dot(pick, got.reshape(nz * CAP_Z, -1)).astype(BF16)
    heads = [packed] + [lax.ppermute(packed, "rank", perm) for perm in sends(ranks)]

    place_z = at_z(place.reshape(NX, nz, slots), my_z)
    owners = place_z[x_order(my_x)].reshape(-1)
    part = dot((row[:, None] == owners[None, :]).astype(BF16), res)
    for head, out in zip(heads, outs):
        part = part + dot(head, out)
    return part.astype(BF16)


def finish(index, part, joins, downs, gain, pack, width):
    place, _, _, bases, passes_first = pack
    ranks, slots = place.shape
    nz = ranks // NX
    block = gain.shape[0]
    rows_z = CAP // nz
    me = lax.axis_index("rank")
    my_x, my_z = lax.div(me, nz), lax.rem(me, nz)
    row = index * CAP + jnp.arange(CAP, dtype=jnp.int32)
    place_z = at_z(place.reshape(NX, nz, slots), my_z)
    order = x_order(my_x)
    base = bases[jnp.where(index < passes_first, 0, 1)]
    got = lax.all_to_all(
        part.reshape(nz, rows_z, block),
        "rank",
        split_axis=0,
        concat_axis=0,
        tiled=True,
        axis_index_groups=groups_z(ranks),
    )
    mixed = jnp.sum(got.astype(F32), axis=0).astype(BF16)
    mixed = lax.all_to_all(
        jnp.broadcast_to(mixed[None], (nz, rows_z, block)),
        "rank",
        split_axis=0,
        concat_axis=0,
        tiled=True,
        axis_index_groups=groups_z(ranks),
    ).reshape(CAP, block)

    wide = mixed.astype(F32)
    square = jnp.sum(wide * wide, axis=1)
    high = lax.reduce_precision(square, 8, 7)
    both = joins[0].shape[0] - EXTRA
    line = jnp.arange(both + EXTRA, dtype=jnp.int32)[:, None]
    extra = jnp.where(line == both, high, jnp.where(line == both + 1, square - high, 0.0))
    scaled = (wide * gain[None, :]).astype(BF16)

    def share(join):
        return (dot_nt(join, scaled) + extra).astype(BF16)

    back = [shift_x(ranks, NX - k) for k in range(1, NX)]
    arrived = [lax.ppermute(share(join), "rank", perm) for join, perm in zip(joins[1:], back)]
    joined = share(joins[0]).astype(F32) + sum(a.astype(F32) for a in arrived)
    factor = lax.rsqrt((joined[both] + joined[both + 1]) / width + 1e-06)[None, :]
    gate, up = joined[: both // 2] * factor, joined[both // 2 : both] * factor
    hidden = (jax.nn.silu(gate) * up).astype(BF16)
    hiddens = [hidden] + [lax.ppermute(hidden, "rank", perm) for perm in sends(ranks)]

    sent = down_rows(hiddens, downs, base - index * CAP)
    got = lax.all_to_all(
        sent,
        "rank",
        split_axis=0,
        concat_axis=0,
        tiled=True,
        axis_index_groups=groups_z(ranks),
    )
    feed = jnp.sum(got.astype(F32), axis=0).astype(BF16)

    inside = (place_z >= index * CAP) & (place_z < (index + 1) * CAP)
    at = jnp.where(inside, place_z - base[my_z], -1).reshape(-1)
    take = (at[:, None] == jnp.arange(CAP_Z, dtype=jnp.int32)[None, :]).astype(BF16)
    keep = (place_z.reshape(-1)[:, None] == row[None, :]).astype(BF16)
    rows = (dot(take, feed) + dot(keep, mixed)).astype(BF16)
    rows = rows.reshape(NX, slots, block)
    pieces = [lax.dynamic_index_in_dim(rows, my_x, 0, False)] + [
        lax.ppermute(
            lax.dynamic_index_in_dim(rows, lax.rem(my_x + k, NX), 0, False),
            "rank",
            shift_x(ranks, k),
        )
        for k in range(1, NX)
    ]
    columns = []
    for x in range(NX):
        column = pieces[0]
        for k in range(1, NX):
            column = jnp.where(order[k] == x, pieces[k], column)
        columns.append(column)
    return jnp.concatenate(columns, axis=1), inside[my_x]


def packing(counts, slots):
    ranks = counts.shape[0]
    nz = ranks // NX
    grid = counts.reshape(NX, nz)
    before = jnp.cumsum(grid, axis=0) - grid
    total = jnp.sum(grid, axis=0)
    first = jnp.minimum(total, CAP_Z)
    rest = total - first
    passes = lax.div(jnp.sum(first) + CAP - 1, CAP)
    base_first = jnp.cumsum(first) - first
    base_rest = passes * CAP + jnp.cumsum(rest) - rest
    slot = jnp.arange(slots, dtype=jnp.int32)
    local = before[:, :, None] + slot
    place = jnp.where(
        local < CAP_Z, base_first[None, :, None] + local, base_rest[None, :, None] + local - CAP_Z
    )
    live = slot < grid[:, :, None]
    place = jnp.where(live, place, -1).reshape(ranks, slots)
    local = jnp.where(live, local, -1)
    counted, bases = jnp.stack([first, rest]), jnp.stack([base_first, base_rest])
    pack = (place, local, counted, bases, passes)
    return pack, passes + lax.div(jnp.sum(rest) + CAP - 1, CAP)


def per_device(
    residual,
    queries,
    latent_cache,
    lengths,
    counts,
    value_up,
    out_proj,
    norm_gain,
    gate_up,
    down_proj,
):
    slots = residual.shape[0]
    ranks = lax.axis_size("rank")
    latent_width, value_width = value_up.shape[1:]
    width = residual.shape[1]
    block = width // NX
    my_x = lax.div(lax.axis_index("rank"), ranks // NX)
    gain = lax.dynamic_slice_in_dim(norm_gain, my_x * block, block, 0).astype(F32)
    member = lax.axis_index("group")
    pack, passes = packing(counts, slots)

    parts, got = exchange_parts([out_proj], [residual], member, block)
    latent = attend(queries, latent_cache, lengths, latent_width, value_width)
    got = lax.optimization_barrier((got, latent))[0]
    value_up = lax.all_gather(
        value_up, "rank", axis=0, tiled=True, axis_index_groups=groups_z(ranks)
    )
    (projs,) = gather_parts(parts, got)
    my_proj = take_cols(out_proj, my_x, block)
    res = [take_cols(residual, my_x, block)] + [g[parts[0] :] for g in got]
    res = jnp.concatenate(res, axis=0)

    each = latent.shape[0] // NX

    def heads_of(x):
        return lax.dynamic_slice_in_dim(latent, x * each, each, 0)

    latents = [heads_of(my_x)] + [
        lax.ppermute(heads_of(lax.rem(my_x + k, NX)), "rank", shift_x(ranks, k))
        for k in range(1, NX)
    ]
    sent = local_values(0, latents, value_up, pack)

    member = lax.optimization_barrier((member, sent))[0]
    parts, got = exchange_parts([gate_up.T, down_proj], [], member, block)
    feeds = gather_parts(parts, got)
    my_join = jnp.pad(take_cols(gate_up.T, my_x, block), ((0, EXTRA), (0, 0)))
    my_down = take_cols(down_proj, my_x, block)

    def run(index, sent):
        part = project(index, sent, res, weight_blocks(my_proj, projs), pack)
        joins = weight_blocks(my_join, feeds[0])
        downs = weight_blocks(my_down, feeds[1])
        return finish(index, part, joins, downs, gain, pack, width)

    def more(state):
        index, out = state
        rows, inside = run(index, local_values(index, latents, value_up, pack))
        return index + 1, jnp.where(inside[:, None], rows, out)

    rows, inside = run(0, sent)
    out = jnp.where(inside[:, None], rows, jnp.zeros((), BF16))
    return lax.while_loop(lambda state: state[0] < passes, more, (jnp.int32(1), out))[1]


def solution(mesh):
    placed = (
        P(("group", "rank"), None),
        P(("group", "rank"), None, None),
        P(("group", "rank"), None, None),
        P(("group", "rank")),
        P("group"),
        P("rank", None, None),
        P("rank", None),
        P(),
        P(None, "rank"),
        P("rank", None),
    )
    return jax.shard_map(
        per_device,
        mesh=mesh,
        in_specs=placed,
        out_specs=P(("group", "rank"), None),
        check_vma=False,
    )
```

```python
import functools

import jax
import jax.numpy as jnp
from jax import lax
from jax.experimental import pallas as pl
from jax.experimental.pallas import tpu as pltpu
from jax.sharding import PartitionSpec as P

F32 = jnp.float32
BF16 = jnp.bfloat16
NX = 4
CAP = 384
CAP_Z = 64
EXTRA = 16
LANES = 128


def shift_x(ranks, k):
    nz = ranks // NX
    return [(x * nz + z, ((x + k) % NX) * nz + z) for x in range(NX) for z in range(nz)]


def shift_z(ranks, k):
    nz = ranks // NX
    return [(x * nz + z, x * nz + (z + k) % nz) for x in range(NX) for z in range(nz)]


def groups_x(ranks):
    nz = ranks // NX
    return [[x * nz + z for x in range(NX)] for z in range(nz)]


def groups_z(ranks):
    nz = ranks // NX
    return [[x * nz + z for z in range(nz)] for x in range(NX)]


def dot(a, b):
    return jnp.dot(a, b, preferred_element_type=F32)


def dot_nt(a, b):
    return lax.dot_general(a, b, (((1,), (1,)), ((), ())), preferred_element_type=F32)


def dot_tn(a, b):
    return lax.dot_general(a, b, (((0,), (0,)), ((), ())), preferred_element_type=F32)


def attend_kernel(scale, step_slots, lengths, queries, keys, out, *scratch):
    step = pl.program_id(0)
    slots, heads = out.shape[1], out.shape[0]
    latent_width = out.shape[2]
    positions = keys.shape[2]
    at = lax.broadcasted_iota(jnp.int32, (heads, positions), 1)
    first = step * step_slots
    scores = [
        jnp.where(at < lengths[first + i], dot(queries[i], keys[i]) * scale, -1e30)
        for i in range(step_slots)
    ]
    scores = jnp.concatenate(scores, axis=0)
    weights = jnp.exp(scores - jnp.max(scores, axis=1, keepdims=True))
    weights = weights * (1.0 / jnp.sum(weights, axis=1, keepdims=True))
    weights = weights.astype(BF16)
    for i in range(step_slots):
        latent = dot_nt(weights[i * heads : (i + 1) * heads], keys[i, :latent_width])
        rows = pl.ds(pl.multiple_of((first + i) * heads, heads), heads)
        for lane, part in enumerate(scratch):
            part[rows, :] = latent[:, lane * LANES : (lane + 1) * LANES]

    @pl.when(step == pl.num_programs(0) - 1)
    def _():
        @pl.loop(0, heads, step=8)
        def _(first):
            for i in range(8):
                rows = [part[pl.ds(first + i, slots, stride=heads), :] for part in scratch]
                out[first + i] = jnp.concatenate(rows, axis=1).astype(BF16)


def attend(queries, latent_cache, lengths, latent_width, value_width):
    slots, heads, key_width = queries.shape
    positions = latent_cache.shape[1]
    rotary_width = key_width - latent_width
    scale = (value_width + rotary_width) ** (-0.5)
    step_slots = 8
    return pl.pallas_call(
        functools.partial(attend_kernel, scale, step_slots),
        out_shape=jax.ShapeDtypeStruct((heads, slots, latent_width), BF16),
        grid=(slots // step_slots,),
        in_specs=[
            pl.BlockSpec(memory_space=pltpu.SMEM),
            pl.BlockSpec((step_slots, heads, key_width), lambda i: (i, 0, 0)),
            pl.BlockSpec((step_slots, key_width, positions), lambda i: (i, 0, 0)),
        ],
        out_specs=pl.BlockSpec((heads, slots, latent_width), lambda i: (0, 0, 0)),
        scratch_shapes=[pltpu.VMEM((slots * heads, LANES), F32)] * (latent_width // LANES),
        compiler_params=pltpu.CompilerParams(vmem_limit_bytes=56 * 2**20),
        cost_estimate=pl.CostEstimate(
            flops=2 * slots * heads * positions * (key_width + latent_width),
            bytes_accessed=2 * slots * (heads + positions) * (key_width + latent_width),
            transcendentals=slots * heads * positions,
        ),
        name="attend",
    )(lengths, queries, latent_cache.transpose(0, 2, 1))


def values_kernel(terms, local, *refs):
    latents, value_up, out = refs[:terms], refs[terms], refs[terms + 1]
    heads = value_up.shape[0]
    value_width = value_up.shape[2]
    blocks, rows, _ = out.shape
    slots = local.shape[1]
    turn = lax.broadcasted_iota(jnp.int32, (rows, slots), 0)
    pick = (turn == local[...]).astype(F32).astype(BF16)
    each = heads // blocks

    @pl.loop(0, blocks)
    def _(block):
        for i in range(each):
            head = block * each + i
            latent = jnp.concatenate([ref[head].astype(F32) for ref in latents], axis=0)
            values = dot(latent.astype(BF16), value_up[head]).astype(BF16)
            columns = slice(i * value_width, (i + 1) * value_width)
            out[block, :, columns] = dot(pick, values).astype(BF16)


def packed_values(latents, value_up, local, blocks):
    heads, slots, latent_width = latents[0].shape
    value_width = value_up.shape[2]
    terms = len(latents)
    macs = terms * slots * heads * (latent_width + CAP_Z) * value_width
    return pl.pallas_call(
        functools.partial(values_kernel, terms),
        out_shape=jax.ShapeDtypeStruct((blocks, CAP_Z, heads // blocks * value_width), BF16),
        in_specs=[pl.BlockSpec(memory_space=pltpu.VMEM)] * (terms + 2),
        out_specs=pl.BlockSpec(memory_space=pltpu.VMEM),
        compiler_params=pltpu.CompilerParams(vmem_limit_bytes=32 * 2**20),
        cost_estimate=pl.CostEstimate(
            flops=2 * macs,
            bytes_accessed=2 * heads * (terms * slots + value_width) * latent_width,
            transcendentals=0,
        ),
        name="packed_values",
    )(local[None], *latents, value_up)


def down_kernel(terms, target, *refs):
    hiddens, downs, out = refs[:terms], refs[terms : 2 * terms], refs[2 * terms]
    total = dot_tn(hiddens[0][...], downs[0][...])
    for hidden, down in zip(hiddens[1:], downs[1:]):
        total = total + dot_tn(hidden[...], down[...])
    total = total.astype(BF16)
    nz, rows, _ = out.shape
    at = lax.broadcasted_iota(jnp.int32, (rows, total.shape[0]), 1)
    turn = lax.broadcasted_iota(jnp.int32, (rows, total.shape[0]), 0)

    @pl.loop(0, nz)
    def _(z):
        pick = (at == turn + target[z]).astype(F32).astype(BF16)
        out[z] = dot(pick, total).astype(BF16)


def down_rows(hiddens, downs, first):
    nz = first.shape[0]
    cap = hiddens[0].shape[1]
    block = downs[0].shape[1]
    terms = len(hiddens)
    depth = sum(h.shape[0] for h in hiddens)
    return pl.pallas_call(
        functools.partial(down_kernel, terms),
        out_shape=jax.ShapeDtypeStruct((nz, CAP_Z, block), BF16),
        in_specs=[pl.BlockSpec(memory_space=pltpu.SMEM)]
        + [pl.BlockSpec(memory_space=pltpu.VMEM)] * (2 * terms),
        out_specs=pl.BlockSpec(memory_space=pltpu.VMEM),
        compiler_params=pltpu.CompilerParams(vmem_limit_bytes=32 * 2**20),
        cost_estimate=pl.CostEstimate(
            flops=2 * cap * block * (depth + nz * CAP_Z),
            bytes_accessed=2 * (depth * (cap + block) + nz * CAP_Z * block),
            transcendentals=0,
        ),
        name="down_rows",
    )(first, *hiddens, *downs)


def sends(ranks):
    return [shift_x(ranks, k) for k in range(1, NX)]


def take_cols(array, index, block):
    return lax.dynamic_slice_in_dim(array, index * block, block, 1)


def part_rows(height, members):
    rows = -(-height // (16 * members)) * 16
    while height % rows:
        rows += 16
    return rows


def exchange_parts(matrices, wholes, member, block):
    ranks = lax.axis_size("rank")
    members = lax.axis_size("group")
    my_x = lax.div(lax.axis_index("rank"), ranks // NX)
    parts = [part_rows(m.shape[0], members) for m in matrices]

    def cut(matrix, rows, x):
        piece = lax.dynamic_slice(matrix, (member * rows, x * block), (rows, block))
        return jnp.where(member * rows < matrix.shape[0], piece, jnp.zeros((), BF16))

    got = []
    for k in range(1, NX):
        x = lax.rem(my_x + k, NX)
        pieces = [cut(m, rows, x) for m, rows in zip(matrices, parts)]
        pieces += [take_cols(m, x, block) for m in wholes]
        got.append(lax.ppermute(jnp.concatenate(pieces, axis=0), "rank", shift_x(ranks, k)))
    return parts, got


def gather_parts(parts, got):
    gathered, first = [], 0
    for rows in parts:
        gathered.append(jnp.stack([g[first : first + rows] for g in got]))
        first += rows
    return [lax.all_gather(g, "group", axis=1, tiled=True) for g in gathered]


def weight_blocks(mine, full):
    height = mine.shape[0]
    full = jnp.pad(full, ((0, 0), (0, max(0, height - full.shape[1])), (0, 0)))
    return [mine] + [full[k, :height] for k in range(NX - 1)]


def x_order(my_x):
    return lax.rem(my_x + NX - jnp.arange(NX, dtype=jnp.int32), NX)


def at_z(array, my_z):
    return lax.dynamic_index_in_dim(array, my_z, 1, False)


def local_values(index, latents, value_up, pack):
    local, _, _, passes_first = pack[1:5]
    ranks = lax.axis_size("rank")
    nz = ranks // NX
    me = lax.axis_index("rank")
    my_x, my_z = lax.div(me, nz), lax.rem(me, nz)
    mine = at_z(local, my_z)[x_order(my_x)].reshape(-1)
    mine = mine - jnp.where(index < passes_first, 0, CAP_Z)
    return packed_values(latents, value_up, mine, nz)


def project(index, sent, res, outs, pack):
    place, _, counted, bases, passes_first = pack
    ranks, slots = place.shape
    nz = ranks // NX
    me = lax.axis_index("rank")
    my_x, my_z = lax.div(me, nz), lax.rem(me, nz)
    row = index * CAP + jnp.arange(CAP, dtype=jnp.int32)
    got = lax.all_to_all(
        sent, "rank", split_axis=0, concat_axis=0, tiled=True, axis_index_groups=groups_z(ranks)
    )

    turn = jnp.arange(CAP_Z, dtype=jnp.int32)
    which = jnp.where(index < passes_first, 0, 1)
    target = jnp.where(turn < counted[which][:, None], bases[which][:, None] + turn, -1)
    pick = (row[:, None] == target.reshape(-1)[None, :]).astype(BF16)
    packed = dot(pick, got.reshape(nz * CAP_Z, -1)).astype(BF16)
    heads = [packed] + [lax.ppermute(packed, "rank", perm) for perm in sends(ranks)]

    place_z = at_z(place.reshape(NX, nz, slots), my_z)
    owners = place_z[x_order(my_x)].reshape(-1)
    part = dot((row[:, None] == owners[None, :]).astype(BF16), res)
    for head, out in zip(heads, outs):
        part = part + dot(head, out)
    return part.astype(BF16)


def finish(index, part, joins, downs, gain, pack, width):
    place, _, _, bases, passes_first = pack
    ranks, slots = place.shape
    nz = ranks // NX
    block = gain.shape[0]
    rows_z = CAP // nz
    me = lax.axis_index("rank")
    my_x, my_z = lax.div(me, nz), lax.rem(me, nz)
    row = index * CAP + jnp.arange(CAP, dtype=jnp.int32)
    place_z = at_z(place.reshape(NX, nz, slots), my_z)
    order = x_order(my_x)
    base = bases[jnp.where(index < passes_first, 0, 1)]
    got = lax.all_to_all(
        part.reshape(nz, rows_z, block),
        "rank",
        split_axis=0,
        concat_axis=0,
        tiled=True,
        axis_index_groups=groups_z(ranks),
    )
    mixed = jnp.sum(got.astype(F32), axis=0).astype(BF16)
    mixed = lax.all_to_all(
        jnp.broadcast_to(mixed[None], (nz, rows_z, block)),
        "rank",
        split_axis=0,
        concat_axis=0,
        tiled=True,
        axis_index_groups=groups_z(ranks),
    ).reshape(CAP, block)

    wide = mixed.astype(F32)
    square = jnp.sum(wide * wide, axis=1)
    high = lax.reduce_precision(square, 8, 7)
    both = joins[0].shape[0] - EXTRA
    line = jnp.arange(both + EXTRA, dtype=jnp.int32)[:, None]
    extra = jnp.where(line == both, high, jnp.where(line == both + 1, square - high, 0.0))
    scaled = (wide * gain[None, :]).astype(BF16)

    def share(join):
        return (dot_nt(join, scaled) + extra).astype(BF16)

    back = [shift_x(ranks, NX - k) for k in range(1, NX)]
    arrived = [lax.ppermute(share(join), "rank", perm) for join, perm in zip(joins[1:], back)]
    joined = share(joins[0]).astype(F32) + sum(a.astype(F32) for a in arrived)
    factor = lax.rsqrt((joined[both] + joined[both + 1]) / width + 1e-06)[None, :]
    gate, up = joined[: both // 2] * factor, joined[both // 2 : both] * factor
    hidden = (jax.nn.silu(gate) * up).astype(BF16)
    hiddens = [hidden] + [lax.ppermute(hidden, "rank", perm) for perm in sends(ranks)]

    sent = down_rows(hiddens, downs, base - index * CAP)
    got = lax.all_to_all(
        sent,
        "rank",
        split_axis=0,
        concat_axis=0,
        tiled=True,
        axis_index_groups=groups_z(ranks),
    )
    feed = jnp.sum(got.astype(F32), axis=0).astype(BF16)

    inside = (place_z >= index * CAP) & (place_z < (index + 1) * CAP)
    at = jnp.where(inside, place_z - base[my_z], -1).reshape(-1)
    take = (at[:, None] == jnp.arange(CAP_Z, dtype=jnp.int32)[None, :]).astype(BF16)
    keep = (place_z.reshape(-1)[:, None] == row[None, :]).astype(BF16)
    rows = (dot(take, feed) + dot(keep, mixed)).astype(BF16)
    rows = rows.reshape(NX, slots, block)
    pieces = [lax.dynamic_index_in_dim(rows, my_x, 0, False)] + [
        lax.ppermute(
            lax.dynamic_index_in_dim(rows, lax.rem(my_x + k, NX), 0, False),
            "rank",
            shift_x(ranks, k),
        )
        for k in range(1, NX)
    ]
    columns = []
    for x in range(NX):
        column = pieces[0]
        for k in range(1, NX):
            column = jnp.where(order[k] == x, pieces[k], column)
        columns.append(column)
    return jnp.concatenate(columns, axis=1), inside[my_x]


def packing(counts, slots):
    ranks = counts.shape[0]
    nz = ranks // NX
    grid = counts.reshape(NX, nz)
    before = jnp.cumsum(grid, axis=0) - grid
    total = jnp.sum(grid, axis=0)
    first = jnp.minimum(total, CAP_Z)
    rest = total - first
    passes = lax.div(jnp.sum(first) + CAP - 1, CAP)
    base_first = jnp.cumsum(first) - first
    base_rest = passes * CAP + jnp.cumsum(rest) - rest
    slot = jnp.arange(slots, dtype=jnp.int32)
    local = before[:, :, None] + slot
    place = jnp.where(
        local < CAP_Z, base_first[None, :, None] + local, base_rest[None, :, None] + local - CAP_Z
    )
    live = slot < grid[:, :, None]
    place = jnp.where(live, place, -1).reshape(ranks, slots)
    local = jnp.where(live, local, -1)
    counted, bases = jnp.stack([first, rest]), jnp.stack([base_first, base_rest])
    pack = (place, local, counted, bases, passes)
    return pack, passes + lax.div(jnp.sum(rest) + CAP - 1, CAP)


def per_device(
    residual,
    queries,
    latent_cache,
    lengths,
    counts,
    value_up,
    out_proj,
    norm_gain,
    gate_up,
    down_proj,
):
    slots = residual.shape[0]
    ranks = lax.axis_size("rank")
    latent_width, value_width = value_up.shape[1:]
    width = residual.shape[1]
    block = width // NX
    my_x = lax.div(lax.axis_index("rank"), ranks // NX)
    gain = lax.dynamic_slice_in_dim(norm_gain, my_x * block, block, 0).astype(F32)
    member = lax.axis_index("group")
    pack, passes = packing(counts, slots)

    parts, got = exchange_parts([out_proj, gate_up.T, down_proj], [residual], member, block)
    latent = attend(queries, latent_cache, lengths, latent_width, value_width)
    got = lax.optimization_barrier((got, latent))[0]
    value_up = lax.all_gather(
        value_up, "rank", axis=0, tiled=True, axis_index_groups=groups_z(ranks)
    )
    projs, *feeds = gather_parts(parts, got)
    my_proj = take_cols(out_proj, my_x, block)
    res = [take_cols(residual, my_x, block)] + [g[sum(parts) :] for g in got]
    res = jnp.concatenate(res, axis=0)

    each = latent.shape[0] // NX

    def heads_of(x):
        return lax.dynamic_slice_in_dim(latent, x * each, each, 0)

    latents = [heads_of(my_x)] + [
        lax.ppermute(heads_of(lax.rem(my_x + k, NX)), "rank", shift_x(ranks, k))
        for k in range(1, NX)
    ]
    sent = local_values(0, latents, value_up, pack)

    my_join = jnp.pad(take_cols(gate_up.T, my_x, block), ((0, EXTRA), (0, 0)))
    my_down = take_cols(down_proj, my_x, block)

    def run(index, sent):
        part = project(index, sent, res, weight_blocks(my_proj, projs), pack)
        joins = weight_blocks(my_join, feeds[0])
        downs = weight_blocks(my_down, feeds[1])
        return finish(index, part, joins, downs, gain, pack, width)

    def more(state):
        index, out = state
        rows, inside = run(index, local_values(index, latents, value_up, pack))
        return index + 1, jnp.where(inside[:, None], rows, out)

    rows, inside = run(0, sent)
    out = jnp.where(inside[:, None], rows, jnp.zeros((), BF16))
    return lax.while_loop(lambda state: state[0] < passes, more, (jnp.int32(1), out))[1]


def solution(mesh):
    placed = (
        P(("group", "rank"), None),
        P(("group", "rank"), None, None),
        P(("group", "rank"), None, None),
        P(("group", "rank")),
        P("group"),
        P("rank", None, None),
        P("rank", None),
        P(),
        P(None, "rank"),
        P("rank", None),
    )
    return jax.shard_map(
        per_device,
        mesh=mesh,
        in_specs=placed,
        out_specs=P(("group", "rank"), None),
        check_vma=False,
    )
```

```python
import functools

import jax
import jax.numpy as jnp
from jax import lax
from jax.experimental import pallas as pl
from jax.experimental.pallas import tpu as pltpu
from jax.sharding import PartitionSpec as P

F32 = jnp.float32
BF16 = jnp.bfloat16
NX = 4
CAP = 384
CAP_Z = 64
EXTRA = 16
LANES = 128


def shift_x(ranks, k):
    nz = ranks // NX
    return [(x * nz + z, ((x + k) % NX) * nz + z) for x in range(NX) for z in range(nz)]


def shift_z(ranks, k):
    nz = ranks // NX
    return [(x * nz + z, x * nz + (z + k) % nz) for x in range(NX) for z in range(nz)]


def groups_x(ranks):
    nz = ranks // NX
    return [[x * nz + z for x in range(NX)] for z in range(nz)]


def groups_z(ranks):
    nz = ranks // NX
    return [[x * nz + z for z in range(nz)] for x in range(NX)]


def dot(a, b):
    return jnp.dot(a, b, preferred_element_type=F32)


def dot_nt(a, b):
    return lax.dot_general(a, b, (((1,), (1,)), ((), ())), preferred_element_type=F32)


def dot_tn(a, b):
    return lax.dot_general(a, b, (((0,), (0,)), ((), ())), preferred_element_type=F32)


def attend_kernel(scale, step_slots, lengths, queries, keys, out, *scratch):
    step = pl.program_id(0)
    slots, heads = out.shape[1], out.shape[0]
    latent_width = out.shape[2]
    positions = keys.shape[2]
    at = lax.broadcasted_iota(jnp.int32, (heads, positions), 1)
    first = step * step_slots
    scores = [
        jnp.where(at < lengths[first + i], dot(queries[i], keys[i]) * scale, -1e30)
        for i in range(step_slots)
    ]
    scores = jnp.concatenate(scores, axis=0)
    weights = jnp.exp(scores - jnp.max(scores, axis=1, keepdims=True))
    weights = weights * (1.0 / jnp.sum(weights, axis=1, keepdims=True))
    weights = weights.astype(BF16)
    for i in range(step_slots):
        latent = dot_nt(weights[i * heads : (i + 1) * heads], keys[i, :latent_width])
        rows = pl.ds(pl.multiple_of((first + i) * heads, heads), heads)
        for lane, part in enumerate(scratch):
            part[rows, :] = latent[:, lane * LANES : (lane + 1) * LANES]

    @pl.when(step == pl.num_programs(0) - 1)
    def _():
        @pl.loop(0, heads, step=8)
        def _(first):
            for i in range(8):
                rows = [part[pl.ds(first + i, slots, stride=heads), :] for part in scratch]
                out[first + i] = jnp.concatenate(rows, axis=1).astype(BF16)


def attend(queries, latent_cache, lengths, latent_width, value_width):
    slots, heads, key_width = queries.shape
    positions = latent_cache.shape[1]
    rotary_width = key_width - latent_width
    scale = (value_width + rotary_width) ** (-0.5)
    step_slots = 8
    return pl.pallas_call(
        functools.partial(attend_kernel, scale, step_slots),
        out_shape=jax.ShapeDtypeStruct((heads, slots, latent_width), BF16),
        grid=(slots // step_slots,),
        in_specs=[
            pl.BlockSpec(memory_space=pltpu.SMEM),
            pl.BlockSpec((step_slots, heads, key_width), lambda i: (i, 0, 0)),
            pl.BlockSpec((step_slots, key_width, positions), lambda i: (i, 0, 0)),
        ],
        out_specs=pl.BlockSpec((heads, slots, latent_width), lambda i: (0, 0, 0)),
        scratch_shapes=[pltpu.VMEM((slots * heads, LANES), F32)] * (latent_width // LANES),
        compiler_params=pltpu.CompilerParams(vmem_limit_bytes=56 * 2**20),
        cost_estimate=pl.CostEstimate(
            flops=2 * slots * heads * positions * (key_width + latent_width),
            bytes_accessed=2 * slots * (heads + positions) * (key_width + latent_width),
            transcendentals=slots * heads * positions,
        ),
        name="attend",
    )(lengths, queries, latent_cache.transpose(0, 2, 1))


def values_kernel(terms, local, *refs):
    latents, value_up, out = refs[:terms], refs[terms], refs[terms + 1]
    heads = value_up.shape[0]
    value_width = value_up.shape[2]
    blocks, rows, _ = out.shape
    slots = local.shape[1]
    turn = lax.broadcasted_iota(jnp.int32, (rows, slots), 0)
    pick = (turn == local[...]).astype(F32).astype(BF16)
    each = heads // blocks

    @pl.loop(0, blocks)
    def _(block):
        for i in range(each):
            head = block * each + i
            latent = jnp.concatenate([ref[head].astype(F32) for ref in latents], axis=0)
            values = dot(latent.astype(BF16), value_up[head]).astype(BF16)
            columns = slice(i * value_width, (i + 1) * value_width)
            out[block, :, columns] = dot(pick, values).astype(BF16)


def packed_values(latents, value_up, local, blocks):
    heads, slots, latent_width = latents[0].shape
    value_width = value_up.shape[2]
    terms = len(latents)
    macs = terms * slots * heads * (latent_width + CAP_Z) * value_width
    return pl.pallas_call(
        functools.partial(values_kernel, terms),
        out_shape=jax.ShapeDtypeStruct((blocks, CAP_Z, heads // blocks * value_width), BF16),
        in_specs=[pl.BlockSpec(memory_space=pltpu.VMEM)] * (terms + 2),
        out_specs=pl.BlockSpec(memory_space=pltpu.VMEM),
        compiler_params=pltpu.CompilerParams(vmem_limit_bytes=32 * 2**20),
        cost_estimate=pl.CostEstimate(
            flops=2 * macs,
            bytes_accessed=2 * heads * (terms * slots + value_width) * latent_width,
            transcendentals=0,
        ),
        name="packed_values",
    )(local[None], *latents, value_up)


def share_kernel(mixed, gain, mine, full, *outs):
    wide = mixed[...].astype(F32)
    both = mine.shape[0]
    squares = wide * wide
    high = squares.astype(BF16)
    low = (squares - high.astype(F32)).astype(BF16)
    ones = jnp.ones((EXTRA, wide.shape[1]), BF16)
    total = dot_nt(ones, high) + dot_nt(ones, low)
    top = total.astype(BF16).astype(F32)
    line = lax.broadcasted_iota(jnp.int32, total.shape, 0)
    extra = jnp.where(line == 0, top, jnp.where(line == 1, total - top, 0.0)).astype(BF16)
    scaled = (wide * gain[...]).astype(BF16)
    for k, out in enumerate(outs):
        join = mine[...] if k == 0 else full[k - 1, :both]
        out[:both] = dot_nt(join, scaled).astype(BF16)
        out[both:] = extra


def gate_up_shares(mixed, gain, mine, full):
    both, block = mine.shape
    cap = mixed.shape[0]
    out = jax.ShapeDtypeStruct((both + EXTRA, cap), BF16)
    return pl.pallas_call(
        share_kernel,
        out_shape=[out] * NX,
        in_specs=[pl.BlockSpec(memory_space=pltpu.VMEM)] * 4,
        out_specs=[pl.BlockSpec(memory_space=pltpu.VMEM)] * NX,
        compiler_params=pltpu.CompilerParams(vmem_limit_bytes=40 * 2**20),
        cost_estimate=pl.CostEstimate(
            flops=2 * NX * both * block * cap,
            bytes_accessed=2 * (cap * block + NX * both * (block + cap)),
            transcendentals=0,
        ),
        name="gate_up_shares",
    )(mixed, gain[None], mine, full)


def down_kernel(terms, target, *refs):
    hiddens, downs, out = refs[:terms], refs[terms : 2 * terms], refs[2 * terms]
    total = dot_tn(hiddens[0][...], downs[0][...])
    for hidden, down in zip(hiddens[1:], downs[1:]):
        total = total + dot_tn(hidden[...], down[...])
    total = total.astype(BF16)
    nz, rows, _ = out.shape
    at = lax.broadcasted_iota(jnp.int32, (rows, total.shape[0]), 1)
    turn = lax.broadcasted_iota(jnp.int32, (rows, total.shape[0]), 0)
    for z in range(nz):
        pick = (at == turn + target[z]).astype(F32).astype(BF16)
        out[z] = dot(pick, total).astype(BF16)


def down_rows(hiddens, downs, first):
    nz = first.shape[0]
    cap = hiddens[0].shape[1]
    block = downs[0].shape[1]
    terms = len(hiddens)
    depth = sum(h.shape[0] for h in hiddens)
    return pl.pallas_call(
        functools.partial(down_kernel, terms),
        out_shape=jax.ShapeDtypeStruct((nz, CAP_Z, block), BF16),
        in_specs=[pl.BlockSpec(memory_space=pltpu.SMEM)]
        + [pl.BlockSpec(memory_space=pltpu.VMEM)] * (2 * terms),
        out_specs=pl.BlockSpec(memory_space=pltpu.VMEM),
        compiler_params=pltpu.CompilerParams(vmem_limit_bytes=32 * 2**20),
        cost_estimate=pl.CostEstimate(
            flops=2 * cap * block * (depth + nz * CAP_Z),
            bytes_accessed=2 * (depth * (cap + block) + nz * CAP_Z * block),
            transcendentals=0,
        ),
        name="down_rows",
    )(first, *hiddens, *downs)


def sends(ranks):
    return [shift_x(ranks, k) for k in range(1, NX)]


def take_cols(array, index, block):
    return lax.dynamic_slice_in_dim(array, index * block, block, 1)


def part_rows(height, members):
    rows = -(-height // (16 * members)) * 16
    while height % rows:
        rows += 16
    return rows


def exchange_parts(matrices, wholes, member, block):
    ranks = lax.axis_size("rank")
    members = lax.axis_size("group")
    my_x = lax.div(lax.axis_index("rank"), ranks // NX)
    parts = [part_rows(m.shape[0], members) for m in matrices]

    def cut(matrix, rows, x):
        return lax.dynamic_slice(matrix, (member * rows, x * block), (rows, block))

    got = []
    for k in range(1, NX):
        x = lax.rem(my_x + k, NX)
        pieces = [cut(m, rows, x) for m, rows in zip(matrices, parts)]
        pieces += [take_cols(m, x, block) for m in wholes]
        got.append(lax.ppermute(jnp.concatenate(pieces, axis=0), "rank", shift_x(ranks, k)))
    return parts, got


def gather_parts(parts, got):
    gathered, first = [], 0
    for rows in parts:
        gathered.append(jnp.stack([g[first : first + rows] for g in got]))
        first += rows
    return [lax.all_gather(g, "group", axis=1, tiled=True) for g in gathered]


def weight_blocks(mine, full):
    return [mine] + [full[k, : mine.shape[0]] for k in range(NX - 1)]


def x_order(my_x):
    return lax.rem(my_x + NX - jnp.arange(NX, dtype=jnp.int32), NX)


def at_z(array, my_z):
    return lax.dynamic_index_in_dim(array, my_z, 1, False)


def local_values(index, latents, value_up, pack):
    local, _, _, passes_first = pack[1:5]
    ranks = lax.axis_size("rank")
    nz = ranks // NX
    me = lax.axis_index("rank")
    my_x, my_z = lax.div(me, nz), lax.rem(me, nz)
    mine = at_z(local, my_z)[x_order(my_x)].reshape(-1)
    mine = mine - jnp.where(index < passes_first, 0, CAP_Z)
    return packed_values(latents, value_up, mine, nz)


def project(index, sent, res, outs, pack):
    place, _, counted, bases, passes_first = pack
    ranks, slots = place.shape
    nz = ranks // NX
    me = lax.axis_index("rank")
    my_x, my_z = lax.div(me, nz), lax.rem(me, nz)
    row = index * CAP + jnp.arange(CAP, dtype=jnp.int32)
    got = lax.all_to_all(
        sent, "rank", split_axis=0, concat_axis=0, tiled=True, axis_index_groups=groups_z(ranks)
    )

    turn = jnp.arange(CAP_Z, dtype=jnp.int32)
    which = jnp.where(index < passes_first, 0, 1)
    target = jnp.where(turn < counted[which][:, None], bases[which][:, None] + turn, -1)
    pick = (row[:, None] == target.reshape(-1)[None, :]).astype(BF16)
    packed = dot(pick, got.reshape(nz * CAP_Z, -1)).astype(BF16)
    heads = [packed] + [lax.ppermute(packed, "rank", perm) for perm in sends(ranks)]

    place_z = at_z(place.reshape(NX, nz, slots), my_z)
    owners = place_z[x_order(my_x)].reshape(-1)
    part = dot((row[:, None] == owners[None, :]).astype(BF16), res)
    for head, out in zip(heads, outs):
        part = part + dot(head, out)
    return part.astype(BF16)


def finish(index, part, my_join, full_join, downs, gain, pack, width):
    place, _, _, bases, passes_first = pack
    ranks, slots = place.shape
    nz = ranks // NX
    block = gain.shape[0]
    rows_z = CAP // nz
    me = lax.axis_index("rank")
    my_x, my_z = lax.div(me, nz), lax.rem(me, nz)
    row = index * CAP + jnp.arange(CAP, dtype=jnp.int32)
    place_z = at_z(place.reshape(NX, nz, slots), my_z)
    order = x_order(my_x)
    base = bases[jnp.where(index < passes_first, 0, 1)]
    got = lax.all_to_all(
        part.reshape(nz, rows_z, block),
        "rank",
        split_axis=0,
        concat_axis=0,
        tiled=True,
        axis_index_groups=groups_z(ranks),
    )
    mixed = jnp.sum(got.astype(F32), axis=0).astype(BF16)
    mixed = lax.all_to_all(
        jnp.broadcast_to(mixed[None], (nz, rows_z, block)),
        "rank",
        split_axis=0,
        concat_axis=0,
        tiled=True,
        axis_index_groups=groups_z(ranks),
    ).reshape(CAP, block)

    shares = gate_up_shares(mixed, gain, my_join, full_join)
    both = my_join.shape[0]
    back = [shift_x(ranks, NX - k) for k in range(1, NX)]
    arrived = [lax.ppermute(share, "rank", perm) for share, perm in zip(shares[1:], back)]
    joined = shares[0].astype(F32) + sum(a.astype(F32) for a in arrived)
    factor = lax.rsqrt((joined[both] + joined[both + 1]) / width + 1e-06)[None, :]
    gate, up = joined[: both // 2] * factor, joined[both // 2 : both] * factor
    hidden = (jax.nn.silu(gate) * up).astype(BF16)
    hiddens = [hidden] + [lax.ppermute(hidden, "rank", perm) for perm in sends(ranks)]

    sent = down_rows(hiddens, downs, base - index * CAP)
    got = lax.all_to_all(
        sent,
        "rank",
        split_axis=0,
        concat_axis=0,
        tiled=True,
        axis_index_groups=groups_z(ranks),
    )
    feed = jnp.sum(got.astype(F32), axis=0).astype(BF16)

    inside = (place_z >= index * CAP) & (place_z < (index + 1) * CAP)
    at = jnp.where(inside, place_z - base[my_z], -1).reshape(-1)
    take = (at[:, None] == jnp.arange(CAP_Z, dtype=jnp.int32)[None, :]).astype(BF16)
    keep = (place_z.reshape(-1)[:, None] == row[None, :]).astype(BF16)
    rows = (dot(take, feed) + dot(keep, mixed)).astype(BF16)
    rows = rows.reshape(NX, slots, block)
    pieces = [lax.dynamic_index_in_dim(rows, my_x, 0, False)] + [
        lax.ppermute(
            lax.dynamic_index_in_dim(rows, lax.rem(my_x + k, NX), 0, False),
            "rank",
            shift_x(ranks, k),
        )
        for k in range(1, NX)
    ]
    columns = []
    for x in range(NX):
        column = pieces[0]
        for k in range(1, NX):
            column = jnp.where(order[k] == x, pieces[k], column)
        columns.append(column)
    return jnp.concatenate(columns, axis=1), inside[my_x]


def packing(counts, slots):
    ranks = counts.shape[0]
    nz = ranks // NX
    grid = counts.reshape(NX, nz)
    before = jnp.cumsum(grid, axis=0) - grid
    total = jnp.sum(grid, axis=0)
    first = jnp.minimum(total, CAP_Z)
    rest = total - first
    passes = lax.div(jnp.sum(first) + CAP - 1, CAP)
    base_first = jnp.cumsum(first) - first
    base_rest = passes * CAP + jnp.cumsum(rest) - rest
    slot = jnp.arange(slots, dtype=jnp.int32)
    local = before[:, :, None] + slot
    place = jnp.where(
        local < CAP_Z, base_first[None, :, None] + local, base_rest[None, :, None] + local - CAP_Z
    )
    live = slot < grid[:, :, None]
    place = jnp.where(live, place, -1).reshape(ranks, slots)
    local = jnp.where(live, local, -1)
    counted, bases = jnp.stack([first, rest]), jnp.stack([base_first, base_rest])
    pack = (place, local, counted, bases, passes)
    return pack, passes + lax.div(jnp.sum(rest) + CAP - 1, CAP)


def per_device(
    residual,
    queries,
    latent_cache,
    lengths,
    counts,
    value_up,
    out_proj,
    norm_gain,
    gate_up,
    down_proj,
):
    slots = residual.shape[0]
    ranks = lax.axis_size("rank")
    latent_width, value_width = value_up.shape[1:]
    width = residual.shape[1]
    block = width // NX
    my_x = lax.div(lax.axis_index("rank"), ranks // NX)
    gain = lax.dynamic_slice_in_dim(norm_gain, my_x * block, block, 0).astype(F32)
    member = lax.axis_index("group")
    pack, passes = packing(counts, slots)

    parts, got = exchange_parts([out_proj, gate_up.T, down_proj], [residual], member, block)
    latent = attend(queries, latent_cache, lengths, latent_width, value_width)
    value_up = lax.all_gather(
        value_up, "rank", axis=0, tiled=True, axis_index_groups=groups_z(ranks)
    )
    each = latent.shape[0] // NX

    def heads_of(x):
        return lax.dynamic_slice_in_dim(latent, x * each, each, 0)

    latents = [heads_of(my_x)] + [
        lax.ppermute(heads_of(lax.rem(my_x + k, NX)), "rank", shift_x(ranks, k))
        for k in range(1, NX)
    ]
    got = lax.optimization_barrier((got, latents))[0]
    projs, *feeds = gather_parts(parts, got)
    my_proj = take_cols(out_proj, my_x, block)
    res = [take_cols(residual, my_x, block)] + [g[sum(parts) :] for g in got]
    res = jnp.concatenate(res, axis=0)

    sent = local_values(0, latents, value_up, pack)
    my_join = take_cols(gate_up.T, my_x, block)
    my_down = take_cols(down_proj, my_x, block)

    def run(index, sent):
        part = project(index, sent, res, weight_blocks(my_proj, projs), pack)
        downs = weight_blocks(my_down, feeds[1])
        return finish(index, part, my_join, feeds[0], downs, gain, pack, width)

    def more(state):
        index, out = state
        rows, inside = run(index, local_values(index, latents, value_up, pack))
        return index + 1, jnp.where(inside[:, None], rows, out)

    rows, inside = run(0, sent)
    out = jnp.where(inside[:, None], rows, jnp.zeros((), BF16))
    return lax.while_loop(lambda state: state[0] < passes, more, (jnp.int32(1), out))[1]


def solution(mesh):
    placed = (
        P(("group", "rank"), None),
        P(("group", "rank"), None, None),
        P(("group", "rank"), None, None),
        P(("group", "rank")),
        P("group"),
        P("rank", None, None),
        P("rank", None),
        P(),
        P(None, "rank"),
        P("rank", None),
    )
    return jax.shard_map(
        per_device,
        mesh=mesh,
        in_specs=placed,
        out_specs=P(("group", "rank"), None),
        check_vma=False,
    )
```

```python
import functools

import jax
import jax.numpy as jnp
from jax import lax
from jax.experimental import pallas as pl
from jax.experimental.pallas import tpu as pltpu
from jax.sharding import PartitionSpec as P

F32 = jnp.float32
BF16 = jnp.bfloat16
NX = 4
CAP = 384
CAP_Z = 64
EXTRA = 16
LANES = 128


def shift_x(ranks, k):
    nz = ranks // NX
    return [(x * nz + z, ((x + k) % NX) * nz + z) for x in range(NX) for z in range(nz)]


def shift_z(ranks, k):
    nz = ranks // NX
    return [(x * nz + z, x * nz + (z + k) % nz) for x in range(NX) for z in range(nz)]


def groups_x(ranks):
    nz = ranks // NX
    return [[x * nz + z for x in range(NX)] for z in range(nz)]


def groups_z(ranks):
    nz = ranks // NX
    return [[x * nz + z for z in range(nz)] for x in range(NX)]


def dot(a, b):
    return jnp.dot(a, b, preferred_element_type=F32)


def dot_nt(a, b):
    return lax.dot_general(a, b, (((1,), (1,)), ((), ())), preferred_element_type=F32)


def dot_tn(a, b):
    return lax.dot_general(a, b, (((0,), (0,)), ((), ())), preferred_element_type=F32)


def attend_kernel(scale, step_slots, lengths, queries, keys, out, *scratch):
    step = pl.program_id(0)
    slots, heads = out.shape[1], out.shape[0]
    latent_width = out.shape[2]
    positions = keys.shape[2]
    at = lax.broadcasted_iota(jnp.int32, (heads, positions), 1)
    first = step * step_slots
    scores = [
        jnp.where(at < lengths[first + i], dot(queries[i], keys[i]) * scale, -1e30)
        for i in range(step_slots)
    ]
    scores = jnp.concatenate(scores, axis=0)
    weights = jnp.exp(scores - jnp.max(scores, axis=1, keepdims=True))
    weights = weights * (1.0 / jnp.sum(weights, axis=1, keepdims=True))
    weights = weights.astype(BF16)
    for i in range(step_slots):
        latent = dot_nt(weights[i * heads : (i + 1) * heads], keys[i, :latent_width])
        rows = pl.ds(pl.multiple_of((first + i) * heads, heads), heads)
        for lane, part in enumerate(scratch):
            part[rows, :] = latent[:, lane * LANES : (lane + 1) * LANES]

    @pl.when(step == pl.num_programs(0) - 1)
    def _():
        @pl.loop(0, heads, step=8)
        def _(first):
            for i in range(8):
                rows = [part[pl.ds(first + i, slots, stride=heads), :] for part in scratch]
                out[first + i] = jnp.concatenate(rows, axis=1).astype(BF16)


def attend(queries, latent_cache, lengths, latent_width, value_width):
    slots, heads, key_width = queries.shape
    positions = latent_cache.shape[1]
    rotary_width = key_width - latent_width
    scale = (value_width + rotary_width) ** (-0.5)
    step_slots = 8
    return pl.pallas_call(
        functools.partial(attend_kernel, scale, step_slots),
        out_shape=jax.ShapeDtypeStruct((heads, slots, latent_width), BF16),
        grid=(slots // step_slots,),
        in_specs=[
            pl.BlockSpec(memory_space=pltpu.SMEM),
            pl.BlockSpec((step_slots, heads, key_width), lambda i: (i, 0, 0)),
            pl.BlockSpec((step_slots, key_width, positions), lambda i: (i, 0, 0)),
        ],
        out_specs=pl.BlockSpec((heads, slots, latent_width), lambda i: (0, 0, 0)),
        scratch_shapes=[pltpu.VMEM((slots * heads, LANES), F32)] * (latent_width // LANES),
        compiler_params=pltpu.CompilerParams(vmem_limit_bytes=56 * 2**20),
        cost_estimate=pl.CostEstimate(
            flops=2 * slots * heads * positions * (key_width + latent_width),
            bytes_accessed=2 * slots * (heads + positions) * (key_width + latent_width),
            transcendentals=slots * heads * positions,
        ),
        name="attend",
    )(lengths, queries, latent_cache.transpose(0, 2, 1))


def values_kernel(terms, local, *refs):
    latents, value_up, out = refs[:terms], refs[terms], refs[terms + 1]
    heads = value_up.shape[0]
    value_width = value_up.shape[2]
    blocks, rows, _ = out.shape
    slots = local.shape[1]
    turn = lax.broadcasted_iota(jnp.int32, (rows, slots), 0)
    pick = (turn == local[...]).astype(F32).astype(BF16)
    each = heads // blocks

    for head in range(heads):
        latent = jnp.concatenate([ref[head].astype(F32) for ref in latents], axis=0)
        values = dot(latent.astype(BF16), value_up[head]).astype(BF16)
        columns = slice(head % each * value_width, (head % each + 1) * value_width)
        out[head // each, :, columns] = dot(pick, values).astype(BF16)


def packed_values(latents, value_up, local, blocks):
    heads, slots, latent_width = latents[0].shape
    value_width = value_up.shape[2]
    terms = len(latents)
    macs = terms * slots * heads * (latent_width + CAP_Z) * value_width
    return pl.pallas_call(
        functools.partial(values_kernel, terms),
        out_shape=jax.ShapeDtypeStruct((blocks, CAP_Z, heads // blocks * value_width), BF16),
        in_specs=[pl.BlockSpec(memory_space=pltpu.VMEM)] * (terms + 2),
        out_specs=pl.BlockSpec(memory_space=pltpu.VMEM),
        compiler_params=pltpu.CompilerParams(vmem_limit_bytes=32 * 2**20),
        cost_estimate=pl.CostEstimate(
            flops=2 * macs,
            bytes_accessed=2 * heads * (terms * slots + value_width) * latent_width,
            transcendentals=0,
        ),
        name="packed_values",
    )(local[None], *latents, value_up)


def share_kernel(mixed, gain, mine, full, *outs):
    wide = mixed[...].astype(F32)
    both = mine.shape[0]
    squares = wide * wide
    high = squares.astype(BF16)
    low = (squares - high.astype(F32)).astype(BF16)
    ones = jnp.ones((EXTRA, wide.shape[1]), BF16)
    total = dot_nt(ones, high) + dot_nt(ones, low)
    top = total.astype(BF16).astype(F32)
    line = lax.broadcasted_iota(jnp.int32, total.shape, 0)
    extra = jnp.where(line == 0, top, jnp.where(line == 1, total - top, 0.0)).astype(BF16)
    scaled = (wide * gain[...]).astype(BF16)
    for k, out in enumerate(outs):
        join = mine[...] if k == 0 else full[k - 1, :both]
        out[:both] = dot_nt(join, scaled).astype(BF16)
        out[both:] = extra


def gate_up_shares(mixed, gain, mine, full):
    both, block = mine.shape
    cap = mixed.shape[0]
    out = jax.ShapeDtypeStruct((both + EXTRA, cap), BF16)
    return pl.pallas_call(
        share_kernel,
        out_shape=[out] * NX,
        in_specs=[pl.BlockSpec(memory_space=pltpu.VMEM)] * 4,
        out_specs=[pl.BlockSpec(memory_space=pltpu.VMEM)] * NX,
        compiler_params=pltpu.CompilerParams(vmem_limit_bytes=40 * 2**20),
        cost_estimate=pl.CostEstimate(
            flops=2 * NX * both * block * cap,
            bytes_accessed=2 * (cap * block + NX * both * (block + cap)),
            transcendentals=0,
        ),
        name="gate_up_shares",
    )(mixed, gain[None], mine, full)


def down_kernel(terms, target, *refs):
    hiddens, downs, out = refs[:terms], refs[terms : 2 * terms], refs[2 * terms]
    total = dot_tn(hiddens[0][...], downs[0][...])
    for hidden, down in zip(hiddens[1:], downs[1:]):
        total = total + dot_tn(hidden[...], down[...])
    total = total.astype(BF16)
    nz, rows, _ = out.shape
    at = lax.broadcasted_iota(jnp.int32, (rows, total.shape[0]), 1)
    turn = lax.broadcasted_iota(jnp.int32, (rows, total.shape[0]), 0)
    for z in range(nz):
        pick = (at == turn + target[z]).astype(F32).astype(BF16)
        out[z] = dot(pick, total).astype(BF16)


def down_rows(hiddens, downs, first):
    nz = first.shape[0]
    cap = hiddens[0].shape[1]
    block = downs[0].shape[1]
    terms = len(hiddens)
    depth = sum(h.shape[0] for h in hiddens)
    return pl.pallas_call(
        functools.partial(down_kernel, terms),
        out_shape=jax.ShapeDtypeStruct((nz, CAP_Z, block), BF16),
        in_specs=[pl.BlockSpec(memory_space=pltpu.SMEM)]
        + [pl.BlockSpec(memory_space=pltpu.VMEM)] * (2 * terms),
        out_specs=pl.BlockSpec(memory_space=pltpu.VMEM),
        compiler_params=pltpu.CompilerParams(vmem_limit_bytes=32 * 2**20),
        cost_estimate=pl.CostEstimate(
            flops=2 * cap * block * (depth + nz * CAP_Z),
            bytes_accessed=2 * (depth * (cap + block) + nz * CAP_Z * block),
            transcendentals=0,
        ),
        name="down_rows",
    )(first, *hiddens, *downs)


def sends(ranks):
    return [shift_x(ranks, k) for k in range(1, NX)]


def take_cols(array, index, block):
    return lax.dynamic_slice_in_dim(array, index * block, block, 1)


def part_rows(height, members):
    rows = -(-height // (8 * members)) * 8
    while height % rows:
        rows += 8
    return rows


def exchange_parts(matrices, wholes, member, block):
    ranks = lax.axis_size("rank")
    members = lax.axis_size("group")
    my_x = lax.div(lax.axis_index("rank"), ranks // NX)
    parts = [part_rows(m.shape[0], members) for m in matrices]

    def cut(matrix, rows, x):
        return lax.dynamic_slice(matrix, (member * rows, x * block), (rows, block))

    got = []
    for k in range(1, NX):
        x = lax.rem(my_x + k, NX)
        pieces = [cut(m, rows, x) for m, rows in zip(matrices, parts)]
        pieces += [take_cols(m, x, block) for m in wholes]
        got.append(lax.ppermute(jnp.concatenate(pieces, axis=0), "rank", shift_x(ranks, k)))
    return parts, got


def gather_parts(parts, got):
    gathered, first = [], 0
    for rows in parts:
        gathered.append(jnp.stack([g[first : first + rows] for g in got]))
        first += rows
    return [lax.all_gather(g, "group", axis=1, tiled=True) for g in gathered]


def weight_blocks(mine, full):
    return [mine] + [full[k, : mine.shape[0]] for k in range(NX - 1)]


def x_order(my_x):
    return lax.rem(my_x + NX - jnp.arange(NX, dtype=jnp.int32), NX)


def at_z(array, my_z):
    return lax.dynamic_index_in_dim(array, my_z, 1, False)


def local_values(index, latents, value_up, pack):
    local, _, _, passes_first = pack[1:5]
    ranks = lax.axis_size("rank")
    nz = ranks // NX
    me = lax.axis_index("rank")
    my_x, my_z = lax.div(me, nz), lax.rem(me, nz)
    mine = at_z(local, my_z)[x_order(my_x)].reshape(-1)
    mine = mine - jnp.where(index < passes_first, 0, CAP_Z)
    return packed_values(latents, value_up, mine, nz)


def project(index, sent, res, outs, pack):
    place, _, counted, bases, passes_first = pack
    ranks, slots = place.shape
    nz = ranks // NX
    me = lax.axis_index("rank")
    my_x, my_z = lax.div(me, nz), lax.rem(me, nz)
    row = index * CAP + jnp.arange(CAP, dtype=jnp.int32)
    got = lax.all_to_all(
        sent, "rank", split_axis=0, concat_axis=0, tiled=True, axis_index_groups=groups_z(ranks)
    )

    turn = jnp.arange(CAP_Z, dtype=jnp.int32)
    which = jnp.where(index < passes_first, 0, 1)
    target = jnp.where(turn < counted[which][:, None], bases[which][:, None] + turn, -1)
    pick = (row[:, None] == target.reshape(-1)[None, :]).astype(BF16)
    packed = dot(pick, got.reshape(nz * CAP_Z, -1)).astype(BF16)
    heads = [packed] + [lax.ppermute(packed, "rank", perm) for perm in sends(ranks)]

    place_z = at_z(place.reshape(NX, nz, slots), my_z)
    owners = place_z[x_order(my_x)].reshape(-1)
    part = dot((row[:, None] == owners[None, :]).astype(BF16), res)
    for head, out in zip(heads, outs):
        part = part + dot(head, out)
    return part.astype(BF16)


def finish(index, part, my_join, full_join, downs, gain, pack, width):
    place, _, _, bases, passes_first = pack
    ranks, slots = place.shape
    nz = ranks // NX
    block = gain.shape[0]
    rows_z = CAP // nz
    me = lax.axis_index("rank")
    my_x, my_z = lax.div(me, nz), lax.rem(me, nz)
    row = index * CAP + jnp.arange(CAP, dtype=jnp.int32)
    place_z = at_z(place.reshape(NX, nz, slots), my_z)
    order = x_order(my_x)
    base = bases[jnp.where(index < passes_first, 0, 1)]
    got = lax.all_to_all(
        part.reshape(nz, rows_z, block),
        "rank",
        split_axis=0,
        concat_axis=0,
        tiled=True,
        axis_index_groups=groups_z(ranks),
    )
    mixed = jnp.sum(got.astype(F32), axis=0).astype(BF16)
    mixed = lax.all_to_all(
        jnp.broadcast_to(mixed[None], (nz, rows_z, block)),
        "rank",
        split_axis=0,
        concat_axis=0,
        tiled=True,
        axis_index_groups=groups_z(ranks),
    ).reshape(CAP, block)

    shares = gate_up_shares(mixed, gain, my_join, full_join)
    both = my_join.shape[0]
    back = [shift_x(ranks, NX - k) for k in range(1, NX)]
    arrived = [lax.ppermute(share, "rank", perm) for share, perm in zip(shares[1:], back)]
    joined = shares[0].astype(F32) + sum(a.astype(F32) for a in arrived)
    factor = lax.rsqrt((joined[both] + joined[both + 1]) / width + 1e-06)[None, :]
    gate, up = joined[: both // 2] * factor, joined[both // 2 : both] * factor
    hidden = (jax.nn.silu(gate) * up).astype(BF16)
    hiddens = [hidden] + [lax.ppermute(hidden, "rank", perm) for perm in sends(ranks)]

    sent = down_rows(hiddens, downs, base - index * CAP)
    got = lax.all_to_all(
        sent,
        "rank",
        split_axis=0,
        concat_axis=0,
        tiled=True,
        axis_index_groups=groups_z(ranks),
    )
    feed = jnp.sum(got.astype(F32), axis=0).astype(BF16)

    inside = (place_z >= index * CAP) & (place_z < (index + 1) * CAP)
    at = jnp.where(inside, place_z - base[my_z], -1).reshape(-1)
    take = (at[:, None] == jnp.arange(CAP_Z, dtype=jnp.int32)[None, :]).astype(BF16)
    keep = (place_z.reshape(-1)[:, None] == row[None, :]).astype(BF16)
    rows = (dot(take, feed) + dot(keep, mixed)).astype(BF16)
    rows = rows.reshape(NX, slots, block)
    pieces = [lax.dynamic_index_in_dim(rows, my_x, 0, False)] + [
        lax.ppermute(
            lax.dynamic_index_in_dim(rows, lax.rem(my_x + k, NX), 0, False),
            "rank",
            shift_x(ranks, k),
        )
        for k in range(1, NX)
    ]
    columns = []
    for x in range(NX):
        column = pieces[0]
        for k in range(1, NX):
            column = jnp.where(order[k] == x, pieces[k], column)
        columns.append(column)
    return jnp.concatenate(columns, axis=1), inside[my_x]


def packing(counts, slots):
    ranks = counts.shape[0]
    nz = ranks // NX
    grid = counts.reshape(NX, nz)
    before = jnp.cumsum(grid, axis=0) - grid
    total = jnp.sum(grid, axis=0)
    first = jnp.minimum(total, CAP_Z)
    rest = total - first
    passes = lax.div(jnp.sum(first) + CAP - 1, CAP)
    base_first = jnp.cumsum(first) - first
    base_rest = passes * CAP + jnp.cumsum(rest) - rest
    slot = jnp.arange(slots, dtype=jnp.int32)
    local = before[:, :, None] + slot
    place = jnp.where(
        local < CAP_Z, base_first[None, :, None] + local, base_rest[None, :, None] + local - CAP_Z
    )
    live = slot < grid[:, :, None]
    place = jnp.where(live, place, -1).reshape(ranks, slots)
    local = jnp.where(live, local, -1)
    counted, bases = jnp.stack([first, rest]), jnp.stack([base_first, base_rest])
    pack = (place, local, counted, bases, passes)
    return pack, passes + lax.div(jnp.sum(rest) + CAP - 1, CAP)


def per_device(
    residual,
    queries,
    latent_cache,
    lengths,
    counts,
    value_up,
    out_proj,
    norm_gain,
    gate_up,
    down_proj,
):
    slots = residual.shape[0]
    ranks = lax.axis_size("rank")
    latent_width, value_width = value_up.shape[1:]
    width = residual.shape[1]
    block = width // NX
    my_x = lax.div(lax.axis_index("rank"), ranks // NX)
    gain = lax.dynamic_slice_in_dim(norm_gain, my_x * block, block, 0).astype(F32)
    member = lax.axis_index("group")
    pack, passes = packing(counts, slots)

    parts, got = exchange_parts([out_proj, gate_up.T, down_proj], [residual], member, block)
    latent = attend(queries, latent_cache, lengths, latent_width, value_width)
    value_up = lax.all_gather(
        value_up, "rank", axis=0, tiled=True, axis_index_groups=groups_z(ranks)
    )
    got = lax.optimization_barrier((got, latent))[0]

    each = latent.shape[0] // NX

    def heads_of(x):
        return lax.dynamic_slice_in_dim(latent, x * each, each, 0)

    latents = [heads_of(my_x)] + [
        lax.ppermute(heads_of(lax.rem(my_x + k, NX)), "rank", shift_x(ranks, k))
        for k in range(1, NX)
    ]
    projs, *feeds = gather_parts(parts, got)
    my_proj = take_cols(out_proj, my_x, block)
    res = [take_cols(residual, my_x, block)] + [g[sum(parts) :] for g in got]
    res = jnp.concatenate(res, axis=0)

    sent = local_values(0, latents, value_up, pack)
    my_join = take_cols(gate_up.T, my_x, block)
    my_down = take_cols(down_proj, my_x, block)

    def run(index, sent):
        part = project(index, sent, res, weight_blocks(my_proj, projs), pack)
        downs = weight_blocks(my_down, feeds[1])
        return finish(index, part, my_join, feeds[0], downs, gain, pack, width)

    def more(state):
        index, out = state
        rows, inside = run(index, local_values(index, latents, value_up, pack))
        return index + 1, jnp.where(inside[:, None], rows, out)

    rows, inside = run(0, sent)
    out = jnp.where(inside[:, None], rows, jnp.zeros((), BF16))
    return lax.while_loop(lambda state: state[0] < passes, more, (jnp.int32(1), out))[1]


def solution(mesh):
    placed = (
        P(("group", "rank"), None),
        P(("group", "rank"), None, None),
        P(("group", "rank"), None, None),
        P(("group", "rank")),
        P("group"),
        P("rank", None, None),
        P("rank", None),
        P(),
        P(None, "rank"),
        P("rank", None),
    )
    return jax.shard_map(
        per_device,
        mesh=mesh,
        in_specs=placed,
        out_specs=P(("group", "rank"), None),
        check_vma=False,
    )
```

```python
import functools

import jax
import jax.numpy as jnp
from jax import lax
from jax.experimental import pallas as pl
from jax.experimental.pallas import tpu as pltpu
from jax.sharding import PartitionSpec as P

F32 = jnp.float32
BF16 = jnp.bfloat16
NX = 4
CAP = 384
CAP_Z = 64
EXTRA = 16
LANES = 128


def shift_x(ranks, k):
    nz = ranks // NX
    return [(x * nz + z, ((x + k) % NX) * nz + z) for x in range(NX) for z in range(nz)]


def shift_z(ranks, k):
    nz = ranks // NX
    return [(x * nz + z, x * nz + (z + k) % nz) for x in range(NX) for z in range(nz)]


def groups_x(ranks):
    nz = ranks // NX
    return [[x * nz + z for x in range(NX)] for z in range(nz)]


def groups_z(ranks):
    nz = ranks // NX
    return [[x * nz + z for z in range(nz)] for x in range(NX)]


def dot(a, b):
    return jnp.dot(a, b, preferred_element_type=F32)


def dot_nt(a, b):
    return lax.dot_general(a, b, (((1,), (1,)), ((), ())), preferred_element_type=F32)


def dot_tn(a, b):
    return lax.dot_general(a, b, (((0,), (0,)), ((), ())), preferred_element_type=F32)


def attend_kernel(scale, step_slots, lengths, queries, keys, out, *scratch):
    step = pl.program_id(0)
    slots, heads = out.shape[1], out.shape[0]
    latent_width = out.shape[2]
    positions = keys.shape[2]
    at = lax.broadcasted_iota(jnp.int32, (heads, positions), 1)
    first = step * step_slots
    scores = [
        jnp.where(at < lengths[first + i], dot(queries[i], keys[i]) * scale, -1e30)
        for i in range(step_slots)
    ]
    scores = jnp.concatenate(scores, axis=0)
    weights = jnp.exp(scores - jnp.max(scores, axis=1, keepdims=True))
    weights = weights * (1.0 / jnp.sum(weights, axis=1, keepdims=True))
    weights = weights.astype(BF16)
    for i in range(step_slots):
        latent = dot_nt(weights[i * heads : (i + 1) * heads], keys[i, :latent_width])
        rows = pl.ds(pl.multiple_of((first + i) * heads, heads), heads)
        for lane, part in enumerate(scratch):
            part[rows, :] = latent[:, lane * LANES : (lane + 1) * LANES]

    @pl.when(step == pl.num_programs(0) - 1)
    def _():
        @pl.loop(0, heads, step=8)
        def _(first):
            for i in range(8):
                rows = [part[pl.ds(first + i, slots, stride=heads), :] for part in scratch]
                out[first + i] = jnp.concatenate(rows, axis=1).astype(BF16)


def attend(queries, latent_cache, lengths, latent_width, value_width):
    slots, heads, key_width = queries.shape
    positions = latent_cache.shape[1]
    rotary_width = key_width - latent_width
    scale = (value_width + rotary_width) ** (-0.5)
    step_slots = 8
    return pl.pallas_call(
        functools.partial(attend_kernel, scale, step_slots),
        out_shape=jax.ShapeDtypeStruct((heads, slots, latent_width), BF16),
        grid=(slots // step_slots,),
        in_specs=[
            pl.BlockSpec(memory_space=pltpu.SMEM),
            pl.BlockSpec((step_slots, heads, key_width), lambda i: (i, 0, 0)),
            pl.BlockSpec((step_slots, key_width, positions), lambda i: (i, 0, 0)),
        ],
        out_specs=pl.BlockSpec((heads, slots, latent_width), lambda i: (0, 0, 0)),
        scratch_shapes=[pltpu.VMEM((slots * heads, LANES), F32)] * (latent_width // LANES),
        compiler_params=pltpu.CompilerParams(vmem_limit_bytes=56 * 2**20),
        cost_estimate=pl.CostEstimate(
            flops=2 * slots * heads * positions * (key_width + latent_width),
            bytes_accessed=2 * slots * (heads + positions) * (key_width + latent_width),
            transcendentals=slots * heads * positions,
        ),
        name="attend",
    )(lengths, queries, latent_cache.transpose(0, 2, 1))


def values_kernel(terms, local, *refs):
    latents, value_up, out = refs[:terms], refs[terms], refs[terms + 1]
    heads = value_up.shape[0]
    value_width = value_up.shape[2]
    blocks, rows, _ = out.shape
    slots = local.shape[1]
    turn = lax.broadcasted_iota(jnp.int32, (rows, slots), 0)
    pick = (turn == local[...]).astype(F32).astype(BF16)
    each = heads // blocks

    for head in range(heads):
        latent = jnp.concatenate([ref[head].astype(F32) for ref in latents], axis=0)
        values = dot(latent.astype(BF16), value_up[head]).astype(BF16)
        columns = slice(head % each * value_width, (head % each + 1) * value_width)
        out[head // each, :, columns] = dot(pick, values).astype(BF16)


def packed_values(latents, value_up, local, blocks):
    heads, slots, latent_width = latents[0].shape
    value_width = value_up.shape[2]
    terms = len(latents)
    macs = terms * slots * heads * (latent_width + CAP_Z) * value_width
    return pl.pallas_call(
        functools.partial(values_kernel, terms),
        out_shape=jax.ShapeDtypeStruct((blocks, CAP_Z, heads // blocks * value_width), BF16),
        in_specs=[pl.BlockSpec(memory_space=pltpu.VMEM)] * (terms + 2),
        out_specs=pl.BlockSpec(memory_space=pltpu.VMEM),
        compiler_params=pltpu.CompilerParams(vmem_limit_bytes=32 * 2**20),
        cost_estimate=pl.CostEstimate(
            flops=2 * macs,
            bytes_accessed=2 * heads * (terms * slots + value_width) * latent_width,
            transcendentals=0,
        ),
        name="packed_values",
    )(local[None], *latents, value_up)


def share_kernel(mixed, gain, mine, full, *outs):
    wide = mixed[...].astype(F32)
    both = mine.shape[0]
    squares = wide * wide
    high = squares.astype(BF16)
    low = (squares - high.astype(F32)).astype(BF16)
    ones = jnp.ones((EXTRA, wide.shape[1]), BF16)
    total = dot_nt(ones, high) + dot_nt(ones, low)
    top = total.astype(BF16).astype(F32)
    line = lax.broadcasted_iota(jnp.int32, total.shape, 0)
    extra = jnp.where(line == 0, top, jnp.where(line == 1, total - top, 0.0)).astype(BF16)
    scaled = (wide * gain[...]).astype(BF16)
    for k, out in enumerate(outs):
        join = mine[...] if k == 0 else full[k - 1, :both]
        out[:both] = dot_nt(join, scaled).astype(BF16)
        out[both:] = extra


def gate_up_shares(mixed, gain, mine, full):
    both, block = mine.shape
    cap = mixed.shape[0]
    out = jax.ShapeDtypeStruct((both + EXTRA, cap), BF16)
    return pl.pallas_call(
        share_kernel,
        out_shape=[out] * NX,
        in_specs=[pl.BlockSpec(memory_space=pltpu.VMEM)] * 4,
        out_specs=[pl.BlockSpec(memory_space=pltpu.VMEM)] * NX,
        compiler_params=pltpu.CompilerParams(vmem_limit_bytes=40 * 2**20),
        cost_estimate=pl.CostEstimate(
            flops=2 * NX * both * block * cap,
            bytes_accessed=2 * (cap * block + NX * both * (block + cap)),
            transcendentals=0,
        ),
        name="gate_up_shares",
    )(mixed, gain[None], mine, full)


def down_kernel(terms, target, *refs):
    hiddens, downs, out = refs[:terms], refs[terms : 2 * terms], refs[2 * terms]
    total = dot_tn(hiddens[0][...], downs[0][...])
    for hidden, down in zip(hiddens[1:], downs[1:]):
        total = total + dot_tn(hidden[...], down[...])
    total = total.astype(BF16)
    nz, rows, _ = out.shape
    at = lax.broadcasted_iota(jnp.int32, (rows, total.shape[0]), 1)
    turn = lax.broadcasted_iota(jnp.int32, (rows, total.shape[0]), 0)
    for z in range(nz):
        pick = (at == turn + target[z]).astype(F32).astype(BF16)
        out[z] = dot(pick, total).astype(BF16)


def down_rows(hiddens, downs, first):
    nz = first.shape[0]
    cap = hiddens[0].shape[1]
    block = downs[0].shape[1]
    terms = len(hiddens)
    depth = sum(h.shape[0] for h in hiddens)
    return pl.pallas_call(
        functools.partial(down_kernel, terms),
        out_shape=jax.ShapeDtypeStruct((nz, CAP_Z, block), BF16),
        in_specs=[pl.BlockSpec(memory_space=pltpu.SMEM)]
        + [pl.BlockSpec(memory_space=pltpu.VMEM)] * (2 * terms),
        out_specs=pl.BlockSpec(memory_space=pltpu.VMEM),
        compiler_params=pltpu.CompilerParams(vmem_limit_bytes=32 * 2**20),
        cost_estimate=pl.CostEstimate(
            flops=2 * cap * block * (depth + nz * CAP_Z),
            bytes_accessed=2 * (depth * (cap + block) + nz * CAP_Z * block),
            transcendentals=0,
        ),
        name="down_rows",
    )(first, *hiddens, *downs)


def sends(ranks):
    return [shift_x(ranks, k) for k in range(1, NX)]


def take_cols(array, index, block):
    return lax.dynamic_slice_in_dim(array, index * block, block, 1)


def part_rows(height, members):
    rows = -(-height // (8 * members)) * 8
    while height % rows:
        rows += 8
    return rows


def exchange_parts(matrices, wholes, member, block):
    ranks = lax.axis_size("rank")
    members = lax.axis_size("group")
    my_x = lax.div(lax.axis_index("rank"), ranks // NX)
    parts = [part_rows(m.shape[0], members) for m in matrices]

    def cut(matrix, rows, x):
        return lax.dynamic_slice(matrix, (member * rows, x * block), (rows, block))

    got = []
    for k in range(1, NX):
        x = lax.rem(my_x + k, NX)
        pieces = [cut(m, rows, x) for m, rows in zip(matrices, parts)]
        pieces += [take_cols(m, x, block) for m in wholes]
        got.append(lax.ppermute(jnp.concatenate(pieces, axis=0), "rank", shift_x(ranks, k)))
    return parts, got


def gather_parts(parts, got):
    gathered, first = [], 0
    for rows in parts:
        gathered.append(jnp.stack([g[first : first + rows] for g in got]))
        first += rows
    return [lax.all_gather(g, "group", axis=1, tiled=True) for g in gathered]


def weight_blocks(mine, full):
    return [mine] + [full[k, : mine.shape[0]] for k in range(NX - 1)]


def x_order(my_x):
    return lax.rem(my_x + NX - jnp.arange(NX, dtype=jnp.int32), NX)


def at_z(array, my_z):
    return lax.dynamic_index_in_dim(array, my_z, 1, False)


def local_values(index, latents, value_up, pack):
    local, _, _, passes_first = pack[1:5]
    ranks = lax.axis_size("rank")
    nz = ranks // NX
    me = lax.axis_index("rank")
    my_x, my_z = lax.div(me, nz), lax.rem(me, nz)
    mine = at_z(local, my_z)[x_order(my_x)].reshape(-1)
    mine = mine - jnp.where(index < passes_first, 0, CAP_Z)
    return packed_values(latents, value_up, mine, nz)


def project(index, sent, res, outs, pack):
    place, _, counted, bases, passes_first = pack
    ranks, slots = place.shape
    nz = ranks // NX
    me = lax.axis_index("rank")
    my_x, my_z = lax.div(me, nz), lax.rem(me, nz)
    row = index * CAP + jnp.arange(CAP, dtype=jnp.int32)
    got = lax.all_to_all(
        sent, "rank", split_axis=0, concat_axis=0, tiled=True, axis_index_groups=groups_z(ranks)
    )

    turn = jnp.arange(CAP_Z, dtype=jnp.int32)
    which = jnp.where(index < passes_first, 0, 1)
    target = jnp.where(turn < counted[which][:, None], bases[which][:, None] + turn, -1)
    pick = (row[:, None] == target.reshape(-1)[None, :]).astype(BF16)
    packed = dot(pick, got.reshape(nz * CAP_Z, -1)).astype(BF16)
    heads = [packed] + [lax.ppermute(packed, "rank", perm) for perm in sends(ranks)]

    place_z = at_z(place.reshape(NX, nz, slots), my_z)
    owners = place_z[x_order(my_x)].reshape(-1)
    part = dot((row[:, None] == owners[None, :]).astype(BF16), res)
    for head, out in zip(heads, outs):
        part = part + dot(head, out)
    return part.astype(BF16)


def finish(index, part, my_join, full_join, downs, gain, pack, width):
    place, _, _, bases, passes_first = pack
    ranks, slots = place.shape
    nz = ranks // NX
    block = gain.shape[0]
    rows_z = CAP // nz
    me = lax.axis_index("rank")
    my_x, my_z = lax.div(me, nz), lax.rem(me, nz)
    row = index * CAP + jnp.arange(CAP, dtype=jnp.int32)
    place_z = at_z(place.reshape(NX, nz, slots), my_z)
    order = x_order(my_x)
    base = bases[jnp.where(index < passes_first, 0, 1)]
    got = lax.all_to_all(
        part.reshape(nz, rows_z, block),
        "rank",
        split_axis=0,
        concat_axis=0,
        tiled=True,
        axis_index_groups=groups_z(ranks),
    )
    mixed = jnp.sum(got.astype(F32), axis=0).astype(BF16)
    mixed = lax.all_to_all(
        jnp.broadcast_to(mixed[None], (nz, rows_z, block)),
        "rank",
        split_axis=0,
        concat_axis=0,
        tiled=True,
        axis_index_groups=groups_z(ranks),
    ).reshape(CAP, block)

    shares = gate_up_shares(mixed, gain, my_join, full_join)
    both = my_join.shape[0]
    back = [shift_x(ranks, NX - k) for k in range(1, NX)]
    arrived = [lax.ppermute(share, "rank", perm) for share, perm in zip(shares[1:], back)]
    joined = shares[0].astype(F32) + sum(a.astype(F32) for a in arrived)
    factor = lax.rsqrt((joined[both] + joined[both + 1]) / width + 1e-06)[None, :]
    gate, up = joined[: both // 2] * factor, joined[both // 2 : both] * factor
    hidden = (jax.nn.silu(gate) * up).astype(BF16)
    hiddens = [hidden] + [lax.ppermute(hidden, "rank", perm) for perm in sends(ranks)]

    sent = down_rows(hiddens, downs, base - index * CAP)
    got = lax.all_to_all(
        sent,
        "rank",
        split_axis=0,
        concat_axis=0,
        tiled=True,
        axis_index_groups=groups_z(ranks),
    )
    feed = jnp.sum(got.astype(F32), axis=0).astype(BF16)

    inside = (place_z >= index * CAP) & (place_z < (index + 1) * CAP)
    at = jnp.where(inside, place_z - base[my_z], -1).reshape(-1)
    take = (at[:, None] == jnp.arange(CAP_Z, dtype=jnp.int32)[None, :]).astype(BF16)
    keep = (place_z.reshape(-1)[:, None] == row[None, :]).astype(BF16)
    rows = (dot(take, feed) + dot(keep, mixed)).astype(BF16)
    rows = rows.reshape(NX, slots, block)
    pieces = [lax.dynamic_index_in_dim(rows, my_x, 0, False)] + [
        lax.ppermute(
            lax.dynamic_index_in_dim(rows, lax.rem(my_x + k, NX), 0, False),
            "rank",
            shift_x(ranks, k),
        )
        for k in range(1, NX)
    ]
    columns = []
    for x in range(NX):
        column = pieces[0]
        for k in range(1, NX):
            column = jnp.where(order[k] == x, pieces[k], column)
        columns.append(column)
    return jnp.concatenate(columns, axis=1), inside[my_x]


def packing(counts, slots):
    ranks = counts.shape[0]
    nz = ranks // NX
    grid = counts.reshape(NX, nz)
    before = jnp.cumsum(grid, axis=0) - grid
    total = jnp.sum(grid, axis=0)
    first = jnp.minimum(total, CAP_Z)
    rest = total - first
    passes = lax.div(jnp.sum(first) + CAP - 1, CAP)
    base_first = jnp.cumsum(first) - first
    base_rest = passes * CAP + jnp.cumsum(rest) - rest
    slot = jnp.arange(slots, dtype=jnp.int32)
    local = before[:, :, None] + slot
    place = jnp.where(
        local < CAP_Z, base_first[None, :, None] + local, base_rest[None, :, None] + local - CAP_Z
    )
    live = slot < grid[:, :, None]
    place = jnp.where(live, place, -1).reshape(ranks, slots)
    local = jnp.where(live, local, -1)
    counted, bases = jnp.stack([first, rest]), jnp.stack([base_first, base_rest])
    pack = (place, local, counted, bases, passes)
    return pack, passes + lax.div(jnp.sum(rest) + CAP - 1, CAP)


def per_device(
    residual,
    queries,
    latent_cache,
    lengths,
    counts,
    value_up,
    out_proj,
    norm_gain,
    gate_up,
    down_proj,
):
    slots = residual.shape[0]
    ranks = lax.axis_size("rank")
    latent_width, value_width = value_up.shape[1:]
    width = residual.shape[1]
    block = width // NX
    my_x = lax.div(lax.axis_index("rank"), ranks // NX)
    gain = lax.dynamic_slice_in_dim(norm_gain, my_x * block, block, 0).astype(F32)
    member = lax.axis_index("group")
    pack, passes = packing(counts, slots)

    parts, got = exchange_parts([out_proj, gate_up.T, down_proj], [residual], member, block)
    latent = attend(queries, latent_cache, lengths, latent_width, value_width)
    value_up = lax.all_gather(
        value_up, "rank", axis=0, tiled=True, axis_index_groups=groups_z(ranks)
    )
    got = lax.optimization_barrier((got, latent))[0]

    each = latent.shape[0] // NX

    def heads_of(x):
        return lax.dynamic_slice_in_dim(latent, x * each, each, 0)

    latents = [heads_of(my_x)] + [
        lax.ppermute(heads_of(lax.rem(my_x + k, NX)), "rank", shift_x(ranks, k))
        for k in range(1, NX)
    ]
    (projs,) = gather_parts(parts[:1], got)
    late = lax.optimization_barrier(([g[parts[0] : sum(parts)] for g in got], latents[1]))[0]
    feeds = gather_parts(parts[1:], late)
    my_proj = take_cols(out_proj, my_x, block)
    res = [take_cols(residual, my_x, block)] + [g[sum(parts) :] for g in got]
    res = jnp.concatenate(res, axis=0)

    sent = local_values(0, latents, value_up, pack)
    my_join = take_cols(gate_up.T, my_x, block)
    my_down = take_cols(down_proj, my_x, block)

    def run(index, sent):
        part = project(index, sent, res, weight_blocks(my_proj, projs), pack)
        downs = weight_blocks(my_down, feeds[1])
        return finish(index, part, my_join, feeds[0], downs, gain, pack, width)

    def more(state):
        index, out = state
        rows, inside = run(index, local_values(index, latents, value_up, pack))
        return index + 1, jnp.where(inside[:, None], rows, out)

    rows, inside = run(0, sent)
    out = jnp.where(inside[:, None], rows, jnp.zeros((), BF16))
    return lax.while_loop(lambda state: state[0] < passes, more, (jnp.int32(1), out))[1]


def solution(mesh):
    placed = (
        P(("group", "rank"), None),
        P(("group", "rank"), None, None),
        P(("group", "rank"), None, None),
        P(("group", "rank")),
        P("group"),
        P("rank", None, None),
        P("rank", None),
        P(),
        P(None, "rank"),
        P("rank", None),
    )
    return jax.shard_map(
        per_device,
        mesh=mesh,
        in_specs=placed,
        out_specs=P(("group", "rank"), None),
        check_vma=False,
    )
```
